32 devices in a mesh: ctx: 8 (over z, y), head: 4 (over x, core).
Axes of the slice: x: 2, y: 2, z: 4, core: 2. Of those that a mesh axis runs over, the one named last changes fastest.
Arguments:
- tokens: bfloat16 [2, 1024, 4096], P(None, 'ctx', 'head'), may hold values from -6 to 6
- w_query: bfloat16 [4096, 2048], P('ctx', 'head'), may hold values from -0.09375 to 0.09375
- w_key: bfloat16 [4096, 2048], P('ctx', 'head'), may hold values from -0.09375 to 0.09375
- w_value: bfloat16 [4096, 2048], P('ctx', 'head'), may hold values from -0.09375 to 0.09375
- norm_gain: float32 [2048], P('head'), may hold values from 0.1 to 1.9
Outputs:
- attended: bfloat16 [2, 1024, 2048], P(None, 'ctx', 'head')
The draws below stay inside these ranges and needn't reach their ends.
All inputs are finite; a program needn't handle non-finite values.
Results may differ from the reference program's by a relative error of at most 0.0072.
Values may be sent and summed in bfloat16 or wider, within the bound.
A program may use at most 192 MiB of HBM per device.

```python
import jax
import jax.numpy as jnp
from jax import lax

D = 4096
HD = 128
HEADS = 16
SEQS = 2
SPAN = 128
LENGTH = 1024


def shard_levels(rng, dims, cuts, least, largest):
    loudness = 1.0
    for axis_at, parts in cuts:
        draws = jax.random.uniform(jax.random.fold_in(jax.random.fold_in(rng, 6), axis_at), (parts,), jnp.float32, least / len(cuts), largest / len(cuts))
        loudness = loudness * jnp.repeat(jnp.exp(draws), dims[axis_at] // parts).reshape((-1,) + (1,) * (len(dims) - 1 - axis_at))
    return loudness


def gaussian(stream_key, dims, deviation, reach, pieces=(), dtype=jnp.bfloat16):
    result = jax.random.normal(stream_key, dims, jnp.float32) * deviation
    if len(pieces) > 0:
        result = shard_levels(stream_key, dims, pieces, -0.22, 0.18) * result
    return jnp.clip(result, min=-reach, max=reach).astype(dtype)


def setup_inputs(seed: int = 0) -> dict:
    keys = jax.random.split(jax.random.key(seed), 6)
    tokens = gaussian(keys[0], (SEQS, LENGTH, D), 1.0, 6.0, ((1, 8), (2, 4)))
    w_query = gaussian(keys[1], (D, HEADS * HD), D ** -0.5, 0.09375, ((0, 8), (1, 4)))
    w_key = gaussian(keys[2], (D, HEADS * HD), D ** -0.5, 0.09375, ((0, 8), (1, 4)))
    w_value = gaussian(keys[3], (D, HEADS * HD), D ** -0.5, 0.09375, ((0, 8), (1, 4)))
    norm_gain = jnp.clip(1.0 + 0.18 * jax.random.normal(keys[4], (HEADS * HD,), jnp.float32), 0.1, 1.9)
    return {"tokens": tokens, "w_query": w_query, "w_key": w_key, "w_value": w_value, "norm_gain": norm_gain}


def rounded(values):
    return lax.optimization_barrier(values.astype(jnp.bfloat16)).astype(jnp.float32)

def reference(tokens, w_query, w_key, w_value, norm_gain):
    token_rows = tokens.reshape(SEQS * LENGTH, D)
    blocks = LENGTH // SPAN

    def project(weight, gated):
        product = jnp.dot(token_rows, weight, preferred_element_type=jnp.float32)
        if gated:
            product = jax.nn.silu(product)
        product = product.astype(jnp.bfloat16).reshape(SEQS, blocks, SPAN, HEADS, HD)
        return product.transpose(1, 0, 3, 2, 4)
    query = project(w_query, True)
    key_all = project(w_key, True)
    value_all = project(w_value, False)
    positions = jnp.arange(SPAN)
    causal = positions[:, None] >= positions[None, :]
    gain_view = norm_gain.reshape(1, HEADS, 1, HD)

    def advance(carried, inputs):
        query_blk, key_blk, value_blk = inputs
        query_f = query_blk.astype(jnp.float32)
        key_f = key_blk.astype(jnp.float32)
        value_f = value_blk.astype(jnp.float32)
        scores = jnp.einsum('shtd,shud->shtu', query_f, key_f)
        masked = rounded(jnp.where(causal, scores, 0.0))
        local_out = jnp.einsum('shtu,shud->shtd', masked, value_f)
        from_prefix = jnp.einsum('shtd,shde->shte', query_f, rounded(carried))
        total = local_out + from_prefix
        scale_inv = lax.rsqrt(lax.optimization_barrier(jnp.mean(total * total, axis=-1, keepdims=True)) + 1e-06)
        normed = (total * scale_inv * gain_view).astype(jnp.bfloat16)
        states = jnp.einsum('shud,shue->shde', key_f, value_f)
        return (carried + states, normed)
    initial = jnp.zeros((SEQS, HEADS, HD, HD), jnp.float32)
    _, outputs = lax.scan(advance, initial, (query, key_all, value_all))
    return outputs.transpose(1, 0, 3, 2, 4).reshape(SEQS, LENGTH, HEADS * HD)
```

```python
import functools

import jax
import jax.numpy as jnp
from jax import lax
from jax.experimental import pallas as pl
from jax.experimental.pallas import tpu as pltpu
from jax.sharding import PartitionSpec as P

HD = 128
MESH = pl.DeviceIdType.MESH


def entering(part, axis, combine, identity):
    place = lax.axis_index(axis)
    gathered = lax.all_gather(part, axis)
    state = jnp.zeros_like(part) + jnp.asarray(identity, part.dtype)

    def one(hop, state):
        return combine(state, lax.dynamic_index_in_dim(gathered, hop, 0, False))

    return lax.fori_loop(0, place, one, state)


def add_states(earlier, later):
    return earlier + later


def general_body(tokens, w_query, w_key, w_value, norm_gain):
    gathered = lax.all_gather(tokens, "head", axis=2, tiled=True)
    seq_count, span_len, model_dim = gathered.shape
    token_rows = gathered.reshape(seq_count * span_len, model_dim)
    features = w_query.shape[1]
    query_full = lax.all_gather(w_query, "ctx", axis=0, tiled=True)
    query_sum = jnp.dot(token_rows, query_full, preferred_element_type=jnp.float32)
    key_full = lax.all_gather(w_key, "ctx", axis=0, tiled=True)
    key_sum = jnp.dot(token_rows, key_full, preferred_element_type=jnp.float32)
    value_full = lax.all_gather(w_value, "ctx", axis=0, tiled=True)
    value_sum = jnp.dot(token_rows, value_full, preferred_element_type=jnp.float32)
    head_count = features // HD

    def heads_first(projected):
        shaped = projected.astype(jnp.bfloat16).reshape(seq_count, span_len, head_count, HD)
        return shaped.transpose(0, 2, 1, 3)

    query = heads_first(jax.nn.silu(query_sum))
    key_all = heads_first(jax.nn.silu(key_sum))
    value_all = heads_first(value_sum)
    positions = jnp.arange(span_len)
    causal = positions[:, None] >= positions[None, :]
    scores = jnp.einsum("shtd,shud->shtu", query, key_all, preferred_element_type=jnp.float32)
    masked = jnp.where(causal, scores, 0.0).astype(jnp.bfloat16)
    local_out = jnp.einsum("shtu,shud->shtd", masked, value_all, preferred_element_type=jnp.float32)
    states = jnp.einsum("shud,shue->shde", key_all, value_all, preferred_element_type=jnp.float32)
    prefix = entering(states, "ctx", add_states, jnp.zeros_like(states))
    from_prefix = jnp.einsum(
        "shtd,shde->shte", query, prefix.astype(jnp.bfloat16), preferred_element_type=jnp.float32
    )
    total = local_out + from_prefix
    scale_inv = lax.rsqrt(jnp.mean(total * total, axis=-1, keepdims=True) + 1e-06)
    gain_view = norm_gain.reshape(1, head_count, 1, HD)
    normed = total * scale_inv * gain_view
    return normed.transpose(0, 2, 1, 3).reshape(seq_count, span_len, features).astype(jnp.bfloat16)


def silu(u):
    return u / (1.0 + jnp.exp(-u))


def mm(a, b):
    return jnp.dot(a, b, preferred_element_type=jnp.float32)


K, V, Q = 0, 1, 2


def kernel(
    tok_ref, wq_ref, wk_ref, wv_ref, gain_ref, out_ref,
    atok, tok, wpeer, s1_out, s1_in, s2_out, s2_in, acc, proj, state, scan_out, scan_in, total,
    a_send, a_recv, b_send, b_recv, c_send, c_recv, w_send, w_recv,
    s1_send, s1_recv, s2_send, s2_recv, x_send, x_recv,
):
    c, h = lax.axis_index("ctx"), lax.axis_index("head")
    y = lax.rem(c, 2)
    zl = lax.rem(lax.div(c, 2), 2)
    zh = lax.div(c, 4)
    core = lax.rem(h, 2)
    x = lax.div(h, 2)
    c_y, c_l, c_h = c + 1 - 2 * y, c + 2 - 4 * zl, c + 4 - 8 * zh
    c_hy = c_h + 1 - 2 * y
    h_c, h_x = h + 1 - 2 * core, h + 2 - 4 * x
    h_xc = h_x + 1 - 2 * core
    weights = (wk_ref, wv_ref, wq_ref)
    seqs, span, width = tok_ref.shape
    half = width // 2
    rows = seqs * span
    heads = out_ref.shape[2] // HD

    barrier = pltpu.get_barrier_semaphore()
    peers = [(c, h_c), (c, h_x), (c, h_xc), (c_y, h), (c_h, h), (c_hy, h), (c_l, h)]
    for peer in peers:
        pl.semaphore_signal(barrier, inc=1, device_id=peer, device_id_type=MESH)
    pl.semaphore_wait(barrier, len(peers))

    def remote(src, dst, send, recv, peer):
        return pltpu.make_async_remote_copy(
            src_ref=src, dst_ref=dst, send_sem=send, recv_sem=recv, device_id=peer, device_id_type=MESH
        )

    pending = []

    def go(copy):
        copy.start()
        pending.append(copy)
        return copy

    w_copies = [remote(weights[j], wpeer.at[j], w_send.at[j], w_recv.at[j], (c_l, h)) for j in range(3)]

    a_copies = [
        go(remote(tok_ref.at[1 - core], atok.at[h], a_send.at[0], a_recv.at[0], (c, h_c))),
        go(remote(tok_ref.at[core], atok.at[h], a_send.at[1], a_recv.at[1], (c, h_x))),
        go(remote(tok_ref.at[1 - core], atok.at[h], a_send.at[2], a_recv.at[2], (c, h_xc))),
    ]
    go(w_copies[K])
    atok[h] = tok_ref[core]
    for copy in a_copies:
        copy.wait_recv()

    def b_source(zd, yd):
        return atok.at[pl.ds(2 * zd, 2), :, pl.ds(pl.multiple_of(yd * half, half), half)]

    blk = 2 * zh + y
    b_copies = [
        go(remote(b_source(1 - zh, y), tok.at[blk, :, core], b_send.at[0], b_recv.at[0], (c_h, h))),
        go(remote(b_source(1 - zh, 1 - y), tok.at[blk, :, core], b_send.at[1], b_recv.at[1], (c_hy, h))),
        go(remote(b_source(zh, 1 - y), tok.at[blk, :, core], b_send.at[2], b_recv.at[2], (c_y, h))),
    ]
    go(w_copies[V])
    go(w_copies[Q])
    tok[blk, :, core] = b_source(zh, y)[...]

    def share(n, place):
        return go(remote(tok.at[place, :, core], tok.at[place, :, core], c_send.at[n], c_recv.at[n], (c, h_c)))

    c_copies = [share(0, blk)]
    b_copies[2].wait_recv()
    c_copies.append(share(1, 2 * zh + 1 - y))
    b_copies[0].wait_recv()
    c_copies.append(share(2, 2 * (1 - zh) + y))
    b_copies[1].wait_recv()
    c_copies.append(share(3, 2 * (1 - zh) + 1 - y))
    for copy in c_copies:
        copy.wait_recv()

    def partial(place, j):
        mine = tok[place, zl].reshape(rows, half)
        other = tok[place, 1 - zl].reshape(rows, half)
        return mm(mine, weights[j][...]) + mm(other, wpeer[j])

    s1_copies, s2_copies = {}, {}

    def first(j):
        w_copies[j].wait_recv()
        for zd in range(2):
            s1_out[j, zd] = partial(2 * zd + 1 - y, j).astype(jnp.bfloat16)
            s1_copies[j, zd] = go(
                remote(s1_out.at[j, zd], s1_in.at[j, zd], s1_send.at[2 * j + zd], s1_recv.at[2 * j + zd], (c_y, h))
            )
        acc[j, 0] = partial(2 * (1 - zh) + y, j)
        acc[j, 1] = partial(2 * zh + y, j)

    def second(j):
        for zd in range(2):
            s1_copies[j, zd].wait_recv()
        s2_out[j] = (acc[j, 0] + s1_in[j, 1 - zh].astype(jnp.float32)).astype(jnp.bfloat16)
        s2_copies[j] = go(remote(s2_out.at[j], s2_in.at[j], s2_send.at[j], s2_recv.at[j], (c_h, h)))
        acc[j, 1] = acc[j, 1] + s1_in[j, zh].astype(jnp.float32)

    def last(j):
        s2_copies[j].wait_recv()
        u = acc[j, 1] + s2_in[j].astype(jnp.float32)
        if j != V:
            u = silu(u)
        proj[j] = u.astype(jnp.bfloat16)

    def piece(j, s, n):
        return proj[j, s * span:(s + 1) * span, n * HD:(n + 1) * HD]

    pairs = [(s, n) for s in range(seqs) for n in range(heads)]

    first(K)
    first(V)
    second(K)
    first(Q)
    second(V)
    last(K)
    last(V)
    for i, (s, n) in enumerate(pairs):
        state[i] = lax.dot_general(
            piece(K, s, n), piece(V, s, n), (((0,), (0,)), ((), ())), preferred_element_type=jnp.float32
        )

    def send_states(step, peer):
        scan_out[step] = state[...].astype(jnp.bfloat16)
        return go(remote(scan_out.at[step], scan_in.at[step], x_send.at[step], x_recv.at[step], peer))

    x0 = send_states(0, (c_y, h))
    second(Q)
    x0.wait_recv()
    came = scan_in[0].astype(jnp.float32)
    state[...] = state[...] + came
    x1 = send_states(1, (c_l, h))
    before = came * y.astype(jnp.float32)
    x1.wait_recv()
    came = scan_in[1].astype(jnp.float32)
    state[...] = state[...] + came
    x2 = send_states(2, (c_h, h))
    state[...] = before + came * zl.astype(jnp.float32)

    last(Q)
    causal = lax.broadcasted_iota(jnp.int32, (span, span), 0) >= lax.broadcasted_iota(jnp.int32, (span, span), 1)
    for i, (s, n) in enumerate(pairs):
        scores = lax.dot_general(
            piece(Q, s, n), piece(K, s, n), (((1,), (1,)), ((), ())), preferred_element_type=jnp.float32
        )
        masked = jnp.where(causal, scores, 0.0).astype(jnp.bfloat16)
        total[i] = mm(masked, piece(V, s, n))

    x2.wait_recv()
    for i, (s, n) in enumerate(pairs):
        prefix = state[i] + scan_in[2, i].astype(jnp.float32) * zh.astype(jnp.float32)
        sums = total[i] + mm(piece(Q, s, n), prefix.astype(jnp.bfloat16))
        scale_inv = lax.rsqrt(jnp.mean(sums * sums, axis=-1, keepdims=True) + 1e-06)
        gain = gain_ref[:, n * HD:(n + 1) * HD]
        out_ref[s, :, n * HD:(n + 1) * HD] = (sums * scale_inv * gain).astype(jnp.bfloat16)

    for copy in pending:
        copy.wait_send()


def fused_body(tokens, w_query, w_key, w_value, norm_gain):
    seqs, span, width = tokens.shape
    depth, features = w_query.shape
    rows, half, heads = seqs * span, width // 2, features // HD
    bf, f32 = jnp.bfloat16, jnp.float32
    dma = pltpu.SemaphoreType.DMA
    return pl.pallas_call(
        kernel,
        out_shape=jax.ShapeDtypeStruct((seqs, span, features), bf),
        in_specs=[pl.BlockSpec(memory_space=pltpu.VMEM)] * 5,
        out_specs=pl.BlockSpec(memory_space=pltpu.VMEM),
        scratch_shapes=[
            pltpu.VMEM((4, span, width), bf),
            pltpu.VMEM((4, 2, seqs, span, half), bf),
            pltpu.VMEM((3, depth, features), bf),
            pltpu.VMEM((3, 2, rows, features), bf),
            pltpu.VMEM((3, 2, rows, features), bf),
            pltpu.VMEM((3, rows, features), bf),
            pltpu.VMEM((3, rows, features), bf),
            pltpu.VMEM((3, 2, rows, features), f32),
            pltpu.VMEM((3, rows, features), bf),
            pltpu.VMEM((seqs * heads, HD, HD), f32),
            pltpu.VMEM((3, seqs * heads, HD, HD), bf),
            pltpu.VMEM((3, seqs * heads, HD, HD), bf),
            pltpu.VMEM((seqs * heads, span, HD), f32),
            dma((3,)), dma((3,)), dma((3,)), dma((3,)), dma((4,)), dma((4,)), dma((3,)), dma((3,)),
            dma((6,)), dma((6,)), dma((3,)), dma((3,)), dma((3,)), dma((3,)),
        ],
        compiler_params=pltpu.CompilerParams(
            collective_id=0, has_side_effects=True, vmem_limit_bytes=48 * 1024 * 1024
        ),
        cost_estimate=pl.CostEstimate(
            flops=2 * rows * width * 4 * features * 3, bytes_accessed=3 * 2**20, transcendentals=0
        ),
    )(tokens, w_query, w_key, w_value, norm_gain.reshape(1, features))


def solution(mesh):
    in_specs = (
        P(None, "ctx", "head"),
        P("ctx", "head"),
        P("ctx", "head"),
        P("ctx", "head"),
        P("head"),
    )
    out_specs = P(None, "ctx", "head")
    fits = mesh.shape["ctx"] == 8 and mesh.shape["head"] == 4
    body = fused_body if fits else general_body
    return jax.shard_map(body, mesh=mesh, in_specs=in_specs, out_specs=out_specs, check_vma=False)
```

```python
import functools

import jax
import jax.numpy as jnp
from jax import lax
from jax.experimental import pallas as pl
from jax.experimental.pallas import tpu as pltpu
from jax.sharding import PartitionSpec as P

HD = 128
MESH = pl.DeviceIdType.MESH


def entering(part, axis, combine, identity):
    place = lax.axis_index(axis)
    gathered = lax.all_gather(part, axis)
    state = jnp.zeros_like(part) + jnp.asarray(identity, part.dtype)

    def one(hop, state):
        return combine(state, lax.dynamic_index_in_dim(gathered, hop, 0, False))

    return lax.fori_loop(0, place, one, state)


def add_states(earlier, later):
    return earlier + later


def general_body(tokens, w_query, w_key, w_value, norm_gain):
    gathered = lax.all_gather(tokens, "head", axis=2, tiled=True)
    seq_count, span_len, model_dim = gathered.shape
    token_rows = gathered.reshape(seq_count * span_len, model_dim)
    features = w_query.shape[1]
    query_full = lax.all_gather(w_query, "ctx", axis=0, tiled=True)
    query_sum = jnp.dot(token_rows, query_full, preferred_element_type=jnp.float32)
    key_full = lax.all_gather(w_key, "ctx", axis=0, tiled=True)
    key_sum = jnp.dot(token_rows, key_full, preferred_element_type=jnp.float32)
    value_full = lax.all_gather(w_value, "ctx", axis=0, tiled=True)
    value_sum = jnp.dot(token_rows, value_full, preferred_element_type=jnp.float32)
    head_count = features // HD

    def heads_first(projected):
        shaped = projected.astype(jnp.bfloat16).reshape(seq_count, span_len, head_count, HD)
        return shaped.transpose(0, 2, 1, 3)

    query = heads_first(jax.nn.silu(query_sum))
    key_all = heads_first(jax.nn.silu(key_sum))
    value_all = heads_first(value_sum)
    positions = jnp.arange(span_len)
    causal = positions[:, None] >= positions[None, :]
    scores = jnp.einsum("shtd,shud->shtu", query, key_all, preferred_element_type=jnp.float32)
    masked = jnp.where(causal, scores, 0.0).astype(jnp.bfloat16)
    local_out = jnp.einsum("shtu,shud->shtd", masked, value_all, preferred_element_type=jnp.float32)
    states = jnp.einsum("shud,shue->shde", key_all, value_all, preferred_element_type=jnp.float32)
    prefix = entering(states, "ctx", add_states, jnp.zeros_like(states))
    from_prefix = jnp.einsum(
        "shtd,shde->shte", query, prefix.astype(jnp.bfloat16), preferred_element_type=jnp.float32
    )
    total = local_out + from_prefix
    scale_inv = lax.rsqrt(jnp.mean(total * total, axis=-1, keepdims=True) + 1e-06)
    gain_view = norm_gain.reshape(1, head_count, 1, HD)
    normed = total * scale_inv * gain_view
    return normed.transpose(0, 2, 1, 3).reshape(seq_count, span_len, features).astype(jnp.bfloat16)


def silu(u):
    return u / (1.0 + jnp.exp(-u))


def mm(a, b):
    return jnp.dot(a, b, preferred_element_type=jnp.float32)


K, V, Q = 0, 1, 2


def kernel(
    tok_ref, wq_ref, wk_ref, wv_ref, gain_ref, out_ref,
    atok, tok, wown, wpeer, s1_out, s1_in, s2_out, s2_in, acc, proj, state, scan_out, scan_in, total,
    l_sem, a_send, a_recv, b_send, b_recv, c_send, c_recv, d_send, d_recv, w_send, w_recv,
    s1_send, s1_recv, s2_send, s2_recv, x_send, x_recv,
):
    c, h = lax.axis_index("ctx"), lax.axis_index("head")
    y = lax.rem(c, 2)
    zl = lax.rem(lax.div(c, 2), 2)
    zh = lax.div(c, 4)
    core = lax.rem(h, 2)
    x = lax.div(h, 2)
    c_y, c_l, c_h = c + 1 - 2 * y, c + 2 - 4 * zl, c + 4 - 8 * zh
    c_hy = c_h + 1 - 2 * y
    h_c, h_x = h + 1 - 2 * core, h + 2 - 4 * x
    h_xc = h_x + 1 - 2 * core
    weights = (wk_ref, wv_ref, wq_ref)
    seqs, span, width = tok_ref.shape
    half = width // 2
    part = span // 2
    rows = seqs * span
    heads = out_ref.shape[2] // HD

    local = [pltpu.make_async_copy(weights[j], wown.at[j], l_sem.at[j]) for j in range(3)]
    for copy in local:
        copy.start()

    def strip(r):
        return pl.ds(pl.multiple_of(r * part, part), part)

    own_piece = pltpu.make_async_copy(tok_ref.at[core, strip(x)], atok.at[h], l_sem.at[3])
    own_piece.start()

    barrier = pltpu.get_barrier_semaphore()
    peers = [(c, h_c), (c, h_x), (c, h_xc), (c_y, h), (c_h, h), (c_hy, h), (c_l, h)]
    for peer in peers:
        pl.semaphore_signal(barrier, inc=1, device_id=peer, device_id_type=MESH)
    pl.semaphore_wait(barrier, len(peers))

    pending = []

    def go(src, dst, send, recv, peer):
        copy = pltpu.make_async_remote_copy(
            src_ref=src, dst_ref=dst, send_sem=send, recv_sem=recv, device_id=peer, device_id_type=MESH
        )
        copy.start()
        pending.append(copy)
        return copy

    def a_go(n, s, r, peer):
        return go(tok_ref.at[s, strip(r)], atok.at[h], a_send.at[n], a_recv.at[n], peer)

    a_copies = [
        a_go(0, core, 1 - x, (c, h_x)), a_go(1, 1 - core, 1 - x, (c, h_xc)), a_go(2, 1 - core, x, (c, h_c)),
    ]

    def w_go(j):
        return go(weights[j], wpeer.at[j], w_send.at[j], w_recv.at[j], (c_l, h))

    w_copies = [w_go(K)]
    for copy in a_copies:
        copy.wait_recv()
    own_piece.wait()

    def b_source(zd, yd):
        return atok.at[pl.ds(2 * zd, 2), :, pl.ds(pl.multiple_of(yd * half, half), half)]

    def piece_of(place):
        return tok.at[place, :, core, strip(x)]

    blk, blk_y, blk_h, blk_hy = 2 * zh + y, 2 * zh + 1 - y, 2 * (1 - zh) + y, 2 * (1 - zh) + 1 - y

    def b_go(n, zd, yd, peer):
        return go(b_source(zd, yd), piece_of(blk), b_send.at[n], b_recv.at[n], peer)

    b_y = b_go(0, zh, 1 - y, (c_y, h))
    b_h = b_go(1, 1 - zh, y, (c_h, h))
    b_hy = b_go(2, 1 - zh, 1 - y, (c_hy, h))
    w_copies += [w_go(V), w_go(Q)]
    tok[blk, :, core, strip(x)] = b_source(zh, y)[...]

    def c_go(n, place):
        return go(piece_of(place), piece_of(place), c_send.at[n], c_recv.at[n], (c, h_x))

    def d_go(n, place):
        mine = tok.at[place, :, core]
        return go(mine, mine, d_send.at[n], d_recv.at[n], (c, h_c))

    def gather_pair(n, first_place, second_place, first_in, second_in):
        if first_in is not None:
            first_in.wait_recv()
        c0 = c_go(n, first_place)
        second_in.wait_recv()
        c1 = c_go(n + 1, second_place)
        c0.wait_recv()
        d0 = d_go(n, first_place)
        c1.wait_recv()
        d1 = d_go(n + 1, second_place)
        d0.wait_recv()
        d1.wait_recv()

    def partial(place, j):
        mine = tok[place, zl].reshape(rows, half)
        other = tok[place, 1 - zl].reshape(rows, half)
        return mm(mine, wown[j]) + mm(other, wpeer[j])

    s1_copies, s2_copies = {}, {}

    def first(j, slot):
        here, away = (blk, blk_y) if slot else (blk_h, blk_hy)
        s1_out[j, slot] = partial(away, j).astype(jnp.bfloat16)
        n = 2 * j + slot
        s1_copies[j, slot] = go(s1_out.at[j, slot], s1_in.at[j, slot], s1_send.at[n], s1_recv.at[n], (c_y, h))
        acc[j, slot] = partial(here, j)

    def second(j):
        s1_copies[j, 0].wait_recv()
        s2_out[j] = (acc[j, 0] + s1_in[j, 0].astype(jnp.float32)).astype(jnp.bfloat16)
        s2_copies[j] = go(s2_out.at[j], s2_in.at[j], s2_send.at[j], s2_recv.at[j], (c_h, h))
        s1_copies[j, 1].wait_recv()
        acc[j, 1] = acc[j, 1] + s1_in[j, 1].astype(jnp.float32)

    def last(j):
        s2_copies[j].wait_recv()
        u = acc[j, 1] + s2_in[j].astype(jnp.float32)
        if j != V:
            u = silu(u)
        proj[j] = u.astype(jnp.bfloat16)

    def piece(j, s, n):
        return proj[j, s * span:(s + 1) * span, n * HD:(n + 1) * HD]

    pairs = [(s, n) for s in range(seqs) for n in range(heads)]

    gather_pair(0, blk, blk_y, None, b_y)
    for copy in local:
        copy.wait()
    w_copies[K].wait_recv()
    first(K, 1)
    gather_pair(2, blk_h, blk_hy, b_h, b_hy)
    first(K, 0)
    w_copies[V].wait_recv()
    first(V, 0)
    first(V, 1)
    second(K)
    w_copies[Q].wait_recv()
    first(Q, 0)
    first(Q, 1)
    second(V)
    last(K)
    last(V)

    def chunk(s):
        return slice(s * heads, (s + 1) * heads)

    def send_states(step, s, peer):
        scan_out[step, chunk(s)] = state[chunk(s)].astype(jnp.bfloat16)
        place = pl.ds(s * heads, heads)
        n = step * seqs + s
        return go(scan_out.at[step, place], scan_in.at[step, place], x_send.at[n], x_recv.at[n], peer)

    x0, x1, x2 = [], [], []
    for s in range(seqs):
        for n in range(heads):
            state[s * heads + n] = lax.dot_general(
                piece(K, s, n), piece(V, s, n), (((0,), (0,)), ((), ())), preferred_element_type=jnp.float32
            )
        x0.append(send_states(0, s, (c_y, h)))
    second(Q)
    for s in range(seqs):
        x0[s].wait_recv()
        state[chunk(s)] = state[chunk(s)] + scan_in[0, chunk(s)].astype(jnp.float32)
        x1.append(send_states(1, s, (c_l, h)))
    for s in range(seqs):
        x1[s].wait_recv()
        came = scan_in[1, chunk(s)].astype(jnp.float32)
        state[chunk(s)] = state[chunk(s)] + came
        x2.append(send_states(2, s, (c_h, h)))
        state[chunk(s)] = came * zl.astype(jnp.float32) + scan_in[0, chunk(s)].astype(jnp.float32) * y.astype(jnp.float32)

    last(Q)
    causal = lax.broadcasted_iota(jnp.int32, (span, span), 0) >= lax.broadcasted_iota(jnp.int32, (span, span), 1)
    for i, (s, n) in enumerate(pairs):
        scores = lax.dot_general(
            piece(Q, s, n), piece(K, s, n), (((1,), (1,)), ((), ())), preferred_element_type=jnp.float32
        )
        masked = jnp.where(causal, scores, 0.0).astype(jnp.bfloat16)
        total[i] = mm(masked, piece(V, s, n))

    for i, (s, n) in enumerate(pairs):
        if n == 0:
            x2[s].wait_recv()
        prefix = state[i] + scan_in[2, i].astype(jnp.float32) * zh.astype(jnp.float32)
        sums = total[i] + mm(piece(Q, s, n), prefix.astype(jnp.bfloat16))
        scale_inv = lax.rsqrt(jnp.mean(sums * sums, axis=-1, keepdims=True) + 1e-06)
        gain = gain_ref[:, n * HD:(n + 1) * HD]
        out_ref[s, :, n * HD:(n + 1) * HD] = (sums * scale_inv * gain).astype(jnp.bfloat16)

    for copy in pending:
        copy.wait_send()


def fused_body(tokens, w_query, w_key, w_value, norm_gain):
    seqs, span, width = tokens.shape
    depth, features = w_query.shape
    rows, half, heads = seqs * span, width // 2, features // HD
    bf, f32 = jnp.bfloat16, jnp.float32
    dma = pltpu.SemaphoreType.DMA
    sems = [4, 3, 3, 3, 3, 4, 4, 4, 4, 3, 3, 6, 6, 3, 3, 3 * seqs, 3 * seqs]
    return pl.pallas_call(
        kernel,
        out_shape=jax.ShapeDtypeStruct((seqs, span, features), bf),
        in_specs=[pl.BlockSpec(memory_space=pltpu.HBM)] * 4 + [pl.BlockSpec(memory_space=pltpu.VMEM)],
        out_specs=pl.BlockSpec(memory_space=pltpu.VMEM),
        scratch_shapes=[
            pltpu.VMEM((4, span // 2, width), bf),
            pltpu.VMEM((4, 2, seqs, span, half), bf),
            pltpu.VMEM((3, depth, features), bf),
            pltpu.VMEM((3, depth, features), bf),
            pltpu.VMEM((3, 2, rows, features), bf),
            pltpu.VMEM((3, 2, rows, features), bf),
            pltpu.VMEM((3, rows, features), bf),
            pltpu.VMEM((3, rows, features), bf),
            pltpu.VMEM((3, 2, rows, features), f32),
            pltpu.VMEM((3, rows, features), bf),
            pltpu.VMEM((seqs * heads, HD, HD), f32),
            pltpu.VMEM((3, seqs * heads, HD, HD), bf),
            pltpu.VMEM((3, seqs * heads, HD, HD), bf),
            pltpu.VMEM((seqs * heads, span, HD), f32),
        ] + [dma((n,)) for n in sems],
        compiler_params=pltpu.CompilerParams(
            collective_id=0, has_side_effects=True, vmem_limit_bytes=62 * 1024 * 1024
        ),
        cost_estimate=pl.CostEstimate(
            flops=2 * rows * width * 4 * features * 3, bytes_accessed=3 * 2**20, transcendentals=0
        ),
    )(tokens, w_query, w_key, w_value, norm_gain.reshape(1, features))


def solution(mesh):
    in_specs = (
        P(None, "ctx", "head"),
        P("ctx", "head"),
        P("ctx", "head"),
        P("ctx", "head"),
        P("head"),
    )
    out_specs = P(None, "ctx", "head")
    fits = mesh.shape["ctx"] == 8 and mesh.shape["head"] == 4
    body = fused_body if fits else general_body
    return jax.shard_map(body, mesh=mesh, in_specs=in_specs, out_specs=out_specs, check_vma=False)
```

```python
import functools

import jax
import jax.numpy as jnp
from jax import lax
from jax.experimental import pallas as pl
from jax.experimental.pallas import tpu as pltpu
from jax.sharding import PartitionSpec as P

HD = 128
MESH = pl.DeviceIdType.MESH


def entering(part, axis, combine, identity):
    place = lax.axis_index(axis)
    gathered = lax.all_gather(part, axis)
    state = jnp.zeros_like(part) + jnp.asarray(identity, part.dtype)

    def one(hop, state):
        return combine(state, lax.dynamic_index_in_dim(gathered, hop, 0, False))

    return lax.fori_loop(0, place, one, state)


def add_states(earlier, later):
    return earlier + later


def general_body(tokens, w_query, w_key, w_value, norm_gain):
    gathered = lax.all_gather(tokens, "head", axis=2, tiled=True)
    seq_count, span_len, model_dim = gathered.shape
    token_rows = gathered.reshape(seq_count * span_len, model_dim)
    features = w_query.shape[1]
    query_full = lax.all_gather(w_query, "ctx", axis=0, tiled=True)
    query_sum = jnp.dot(token_rows, query_full, preferred_element_type=jnp.float32)
    key_full = lax.all_gather(w_key, "ctx", axis=0, tiled=True)
    key_sum = jnp.dot(token_rows, key_full, preferred_element_type=jnp.float32)
    value_full = lax.all_gather(w_value, "ctx", axis=0, tiled=True)
    value_sum = jnp.dot(token_rows, value_full, preferred_element_type=jnp.float32)
    head_count = features // HD

    def heads_first(projected):
        shaped = projected.astype(jnp.bfloat16).reshape(seq_count, span_len, head_count, HD)
        return shaped.transpose(0, 2, 1, 3)

    query = heads_first(jax.nn.silu(query_sum))
    key_all = heads_first(jax.nn.silu(key_sum))
    value_all = heads_first(value_sum)
    positions = jnp.arange(span_len)
    causal = positions[:, None] >= positions[None, :]
    scores = jnp.einsum("shtd,shud->shtu", query, key_all, preferred_element_type=jnp.float32)
    masked = jnp.where(causal, scores, 0.0).astype(jnp.bfloat16)
    local_out = jnp.einsum("shtu,shud->shtd", masked, value_all, preferred_element_type=jnp.float32)
    states = jnp.einsum("shud,shue->shde", key_all, value_all, preferred_element_type=jnp.float32)
    prefix = entering(states, "ctx", add_states, jnp.zeros_like(states))
    from_prefix = jnp.einsum(
        "shtd,shde->shte", query, prefix.astype(jnp.bfloat16), preferred_element_type=jnp.float32
    )
    total = local_out + from_prefix
    scale_inv = lax.rsqrt(jnp.mean(total * total, axis=-1, keepdims=True) + 1e-06)
    gain_view = norm_gain.reshape(1, head_count, 1, HD)
    normed = total * scale_inv * gain_view
    return normed.transpose(0, 2, 1, 3).reshape(seq_count, span_len, features).astype(jnp.bfloat16)


def silu(u):
    return u / (1.0 + jnp.exp(-u))


def mm(a, b):
    return jnp.dot(a, b, preferred_element_type=jnp.float32)


K, V, Q = 0, 1, 2


def kernel(
    tok_ref, wq_ref, wk_ref, wv_ref, gain_ref, out_ref,
    atok, tok, wown, wpeer, s1_out, s1_in, s2_out, s2_in, acc, proj, state, scan_out, scan_in, sum_out, sum_in,
    total, res_out, res_in,
    l_sem, a_send, a_recv, b_send, b_recv, e_send, e_recv, c_send, c_recv, d_send, d_recv, w_send, w_recv,
    s1_send, s1_recv, s2_send, s2_recv, x_send, x_recv, r_send, r_recv,
):
    c, h = lax.axis_index("ctx"), lax.axis_index("head")
    y = lax.rem(c, 2)
    zl = lax.rem(lax.div(c, 2), 2)
    zh = lax.div(c, 4)
    core = lax.rem(h, 2)
    x = lax.div(h, 2)
    c_y, c_l, c_h = c + 1 - 2 * y, c + 2 - 4 * zl, c + 4 - 8 * zh
    c_hy = c_h + 1 - 2 * y
    h_c, h_x = h + 1 - 2 * core, h + 2 - 4 * x
    h_xc = h_x + 1 - 2 * core
    weights = (wk_ref, wv_ref, wq_ref)
    seqs, span, width = tok_ref.shape
    half = width // 2
    part = span // 2
    rows = seqs * span
    cols = out_ref.shape[2] // 2
    heads = cols // HD

    def col_half(n):
        return pl.ds(pl.multiple_of(n * cols, cols), cols)

    local = [pltpu.make_async_copy(weights[j].at[:, col_half(zl)], wown.at[j], l_sem.at[j]) for j in range(3)]
    for copy in local:
        copy.start()

    def strip(r):
        return pl.ds(pl.multiple_of(r * part, part), part)

    own_piece = pltpu.make_async_copy(tok_ref.at[core, strip(x)], atok.at[h], l_sem.at[3])
    own_piece.start()

    barrier = pltpu.get_barrier_semaphore()
    peers = [(c, h_c), (c, h_x), (c, h_xc), (c_y, h), (c_h, h), (c_hy, h), (c_l, h)]
    for peer in peers:
        pl.semaphore_signal(barrier, inc=1, device_id=peer, device_id_type=MESH)
    pl.semaphore_wait(barrier, len(peers))

    pending = []

    def go(src, dst, send, recv, peer):
        copy = pltpu.make_async_remote_copy(
            src_ref=src, dst_ref=dst, send_sem=send, recv_sem=recv, device_id=peer, device_id_type=MESH
        )
        copy.start()
        pending.append(copy)
        return copy

    def a_go(n, s, r, peer):
        return go(tok_ref.at[s, strip(r)], atok.at[h], a_send.at[n], a_recv.at[n], peer)

    a_copies = [
        a_go(0, core, 1 - x, (c, h_x)), a_go(1, 1 - core, 1 - x, (c, h_xc)), a_go(2, 1 - core, x, (c, h_c)),
    ]

    def w_go(j):
        return go(weights[j].at[:, col_half(1 - zl)], wpeer.at[j], w_send.at[j], w_recv.at[j], (c_l, h))

    w_copies = [w_go(K)]
    for copy in a_copies:
        copy.wait_recv()
    own_piece.wait()

    def b_source(zd, yd):
        return atok.at[pl.ds(2 * zd, 2), :, pl.ds(pl.multiple_of(yd * half, half), half)]

    def piece_of(zp, place):
        return tok.at[zp, place, :, core, strip(x)]

    blk, blk_y, blk_h, blk_hy = 2 * zh + y, 2 * zh + 1 - y, 2 * (1 - zh) + y, 2 * (1 - zh) + 1 - y

    def b_go(n, zd, yd, peer):
        return go(b_source(zd, yd), piece_of(zl, blk), b_send.at[n], b_recv.at[n], peer)

    b_h = b_go(1, 1 - zh, y, (c_h, h))
    b_hy = b_go(2, 1 - zh, 1 - y, (c_hy, h))
    b_y = b_go(0, zh, 1 - y, (c_y, h))
    tok[zl, blk, :, core, strip(x)] = b_source(zh, y)[...]

    places = (blk, blk_y, blk_h, blk_hy)

    def e_go(n):
        mine = piece_of(zl, places[n])
        return go(mine, mine, e_send.at[n], e_recv.at[n], (c_l, h))

    def c_go(n):
        mine = piece_of(zl if n < 4 else 1 - zl, places[n % 4])
        return go(mine, mine, c_send.at[n], c_recv.at[n], (c, h_x))

    def d_go(n):
        mine = tok.at[zl if n < 4 else 1 - zl, places[n % 4], :, core]
        return go(mine, mine, d_send.at[n], d_recv.at[n], (c, h_c))

    def partial(zp, place, j):
        mine = tok[zp, place, zl].reshape(rows, half)
        other = tok[zp, place, 1 - zl].reshape(rows, half)
        return mm(mine, wown[j]) + mm(other, wpeer[j])

    s1_copies, s2_copies = {}, {}

    def first(j, slot):
        here, away = (blk, blk_y) if slot else (blk_h, blk_hy)
        for zp in range(2):
            s1_out[j, slot, zp] = partial(zp, away, j).astype(jnp.bfloat16)
        n = 2 * j + slot
        s1_copies[j, slot] = go(s1_out.at[j, slot], s1_in.at[j, slot], s1_send.at[n], s1_recv.at[n], (c_y, h))
        for zp in range(2):
            acc[j, slot, zp] = partial(zp, here, j)

    def second(j):
        s1_copies[j, 0].wait_recv()
        s2_out[j] = (acc[j, 0] + s1_in[j, 0].astype(jnp.float32)).astype(jnp.bfloat16)
        s2_copies[j] = go(s2_out.at[j], s2_in.at[j], s2_send.at[j], s2_recv.at[j], (c_h, h))

    def last(j):
        s1_copies[j, 1].wait_recv()
        s2_copies[j].wait_recv()
        u = acc[j, 1] + s1_in[j, 1].astype(jnp.float32) + s2_in[j].astype(jnp.float32)
        if j != V:
            u = silu(u)
        proj[j] = u.astype(jnp.bfloat16)

    def piece(j, zp, s, n):
        return proj[j, zp, s * span:(s + 1) * span, n * HD:(n + 1) * HD]

    pairs = [(s, n) for s in range(seqs) for n in range(heads)]

    e, cc, d = {}, {}, {}
    e[0], cc[0] = e_go(0), c_go(0)
    w_copies.append(w_go(V))
    b_y.wait_recv()
    e[1], cc[1] = e_go(1), c_go(1)
    w_copies.append(w_go(Q))
    for n in range(2):
        e[n].wait_recv()
        cc[4 + n] = c_go(4 + n)
    for n in range(2):
        cc[n].wait_recv()
        d[n] = d_go(n)
    for n, came in ((2, b_h), (3, b_hy)):
        came.wait_recv()
        e[n], cc[n] = e_go(n), c_go(n)
    for n in (4, 5):
        cc[n].wait_recv()
        d[n] = d_go(n)
    for n in (2, 3):
        e[n].wait_recv()
        cc[4 + n] = c_go(4 + n)
    for copy in local:
        copy.wait()
    w_copies[K].wait_recv()
    for n in (0, 1, 4, 5):
        d[n].wait_recv()
    first(K, 1)
    for n in (2, 3, 6, 7):
        cc[n].wait_recv()
        d[n] = d_go(n)
    w_copies[V].wait_recv()
    first(V, 1)
    for n in (2, 3, 6, 7):
        d[n].wait_recv()
    first(K, 0)
    first(V, 0)
    w_copies[Q].wait_recv()
    first(Q, 0)
    second(K)
    first(Q, 1)
    second(V)
    second(Q)
    last(K)
    last(V)

    for zp in range(2):
        for i, (s, n) in enumerate(pairs):
            state[zp, i] = lax.dot_general(
                piece(K, zp, s, n), piece(V, zp, s, n), (((0,), (0,)), ((), ())), preferred_element_type=jnp.float32
            )
    scan_out[...] = state[...].astype(jnp.bfloat16)
    x0 = go(scan_out, scan_in, x_send.at[0], x_recv.at[0], (c_y, h))

    causal = lax.broadcasted_iota(jnp.int32, (span, span), 0) >= lax.broadcasted_iota(jnp.int32, (span, span), 1)

    x0.wait_recv()
    both = state[0] + scan_in[0].astype(jnp.float32)
    sum_out[...] = (both + state[1] + scan_in[1].astype(jnp.float32)).astype(jnp.bfloat16)
    x1 = go(sum_out, sum_in, x_send.at[1], x_recv.at[1], (c_h, h))
    is_odd = y.astype(jnp.float32)
    state[0] = scan_in[0].astype(jnp.float32) * is_odd
    state[1] = both + scan_in[1].astype(jnp.float32) * is_odd

    last(Q)
    for zp in range(2):
        for i, (s, n) in enumerate(pairs):
            scores = lax.dot_general(
                piece(Q, zp, s, n), piece(K, zp, s, n), (((1,), (1,)), ((), ())), preferred_element_type=jnp.float32
            )
            masked = jnp.where(causal, scores, 0.0).astype(jnp.bfloat16)
            total[zp, i] = mm(masked, piece(V, zp, s, n))

    x1.wait_recv()

    def finish(zp, i, s, n):
        prefix = state[zp, i] + sum_in[i].astype(jnp.float32) * zh.astype(jnp.float32)
        sums = total[zp, i] + mm(piece(Q, zp, s, n), prefix.astype(jnp.bfloat16))
        scale_inv = lax.rsqrt(jnp.mean(sums * sums, axis=-1, keepdims=True) + 1e-06)
        gain = gain_ref[:, pl.ds(pl.multiple_of(zl * cols + n * HD, HD), HD)]
        return (sums * scale_inv * gain).astype(jnp.bfloat16)

    for i, (s, n) in enumerate(pairs):
        res_out[s, :, n * HD:(n + 1) * HD] = finish(1 - zl, i, s, n)
    res = go(res_out, res_in, r_send.at[0], r_recv.at[0], (c_l, h))
    for i, (s, n) in enumerate(pairs):
        out_ref[s, :, pl.ds(pl.multiple_of(zl * cols + n * HD, HD), HD)] = finish(zl, i, s, n)
    res.wait_recv()
    out_ref[:, :, col_half(1 - zl)] = res_in[...]

    for copy in pending:
        copy.wait_send()


def fused_body(tokens, w_query, w_key, w_value, norm_gain):
    seqs, span, width = tokens.shape
    depth, features = w_query.shape
    rows, half, cols = seqs * span, width // 2, features // 2
    states = seqs * cols // HD
    bf, f32 = jnp.bfloat16, jnp.float32
    dma = pltpu.SemaphoreType.DMA
    sems = [4, 3, 3, 3, 3, 4, 4, 8, 8, 8, 8, 3, 3, 6, 6, 3, 3, 2, 2, 1, 1]
    return pl.pallas_call(
        kernel,
        out_shape=jax.ShapeDtypeStruct((seqs, span, features), bf),
        in_specs=[pl.BlockSpec(memory_space=pltpu.HBM)] * 4 + [pl.BlockSpec(memory_space=pltpu.VMEM)],
        out_specs=pl.BlockSpec(memory_space=pltpu.VMEM),
        scratch_shapes=[
            pltpu.VMEM((4, span // 2, width), bf),
            pltpu.VMEM((2, 4, 2, seqs, span, half), bf),
            pltpu.VMEM((3, depth, cols), bf),
            pltpu.VMEM((3, depth, cols), bf),
            pltpu.VMEM((3, 2, 2, rows, cols), bf),
            pltpu.VMEM((3, 2, 2, rows, cols), bf),
            pltpu.VMEM((3, 2, rows, cols), bf),
            pltpu.VMEM((3, 2, rows, cols), bf),
            pltpu.VMEM((3, 2, 2, rows, cols), f32),
            pltpu.VMEM((3, 2, rows, cols), bf),
            pltpu.VMEM((2, states, HD, HD), f32),
            pltpu.VMEM((2, states, HD, HD), bf),
            pltpu.VMEM((2, states, HD, HD), bf),
            pltpu.VMEM((states, HD, HD), bf),
            pltpu.VMEM((states, HD, HD), bf),
            pltpu.VMEM((2, states, span, HD), f32),
            pltpu.VMEM((seqs, span, cols), bf),
            pltpu.VMEM((seqs, span, cols), bf),
        ] + [dma((n,)) for n in sems],
        compiler_params=pltpu.CompilerParams(
            collective_id=0, has_side_effects=True, vmem_limit_bytes=62 * 1024 * 1024
        ),
        cost_estimate=pl.CostEstimate(
            flops=2 * rows * width * 4 * features * 3, bytes_accessed=3 * 2**20, transcendentals=0
        ),
    )(tokens, w_query, w_key, w_value, norm_gain.reshape(1, features))


def solution(mesh):
    in_specs = (
        P(None, "ctx", "head"),
        P("ctx", "head"),
        P("ctx", "head"),
        P("ctx", "head"),
        P("head"),
    )
    out_specs = P(None, "ctx", "head")
    fits = mesh.shape["ctx"] == 8 and mesh.shape["head"] == 4
    body = fused_body if fits else general_body
    return jax.shard_map(body, mesh=mesh, in_specs=in_specs, out_specs=out_specs, check_vma=False)
```

```python
import functools

import jax
import jax.numpy as jnp
from jax import lax
from jax.experimental import pallas as pl
from jax.experimental.pallas import tpu as pltpu
from jax.sharding import PartitionSpec as P

HD = 128
MESH = pl.DeviceIdType.MESH


def entering(part, axis, combine, identity):
    place = lax.axis_index(axis)
    gathered = lax.all_gather(part, axis)
    state = jnp.zeros_like(part) + jnp.asarray(identity, part.dtype)

    def one(hop, state):
        return combine(state, lax.dynamic_index_in_dim(gathered, hop, 0, False))

    return lax.fori_loop(0, place, one, state)


def add_states(earlier, later):
    return earlier + later


def general_body(tokens, w_query, w_key, w_value, norm_gain):
    gathered = lax.all_gather(tokens, "head", axis=2, tiled=True)
    seq_count, span_len, model_dim = gathered.shape
    token_rows = gathered.reshape(seq_count * span_len, model_dim)
    features = w_query.shape[1]
    query_full = lax.all_gather(w_query, "ctx", axis=0, tiled=True)
    query_sum = jnp.dot(token_rows, query_full, preferred_element_type=jnp.float32)
    key_full = lax.all_gather(w_key, "ctx", axis=0, tiled=True)
    key_sum = jnp.dot(token_rows, key_full, preferred_element_type=jnp.float32)
    value_full = lax.all_gather(w_value, "ctx", axis=0, tiled=True)
    value_sum = jnp.dot(token_rows, value_full, preferred_element_type=jnp.float32)
    head_count = features // HD

    def heads_first(projected):
        shaped = projected.astype(jnp.bfloat16).reshape(seq_count, span_len, head_count, HD)
        return shaped.transpose(0, 2, 1, 3)

    query = heads_first(jax.nn.silu(query_sum))
    key_all = heads_first(jax.nn.silu(key_sum))
    value_all = heads_first(value_sum)
    positions = jnp.arange(span_len)
    causal = positions[:, None] >= positions[None, :]
    scores = jnp.einsum("shtd,shud->shtu", query, key_all, preferred_element_type=jnp.float32)
    masked = jnp.where(causal, scores, 0.0).astype(jnp.bfloat16)
    local_out = jnp.einsum("shtu,shud->shtd", masked, value_all, preferred_element_type=jnp.float32)
    states = jnp.einsum("shud,shue->shde", key_all, value_all, preferred_element_type=jnp.float32)
    prefix = entering(states, "ctx", add_states, jnp.zeros_like(states))
    from_prefix = jnp.einsum(
        "shtd,shde->shte", query, prefix.astype(jnp.bfloat16), preferred_element_type=jnp.float32
    )
    total = local_out + from_prefix
    scale_inv = lax.rsqrt(jnp.mean(total * total, axis=-1, keepdims=True) + 1e-06)
    gain_view = norm_gain.reshape(1, head_count, 1, HD)
    normed = total * scale_inv * gain_view
    return normed.transpose(0, 2, 1, 3).reshape(seq_count, span_len, features).astype(jnp.bfloat16)


def silu(u):
    return u / (1.0 + jnp.exp(-u))


def mm(a, b):
    return jnp.dot(a, b, preferred_element_type=jnp.float32)


K, V, Q = 0, 1, 2


def kernel(
    tok_ref, wq_ref, wk_ref, wv_ref, gain_ref, out_ref,
    atok, tok, wown, wpeer, s1_out, s1_in, s2_out, s2_in, acc, proj, state, scan_out, scan_in, total,
    l_sem, a_send, a_recv, b_send, b_recv, c_send, c_recv, d_send, d_recv, w_send, w_recv,
    s1_send, s1_recv, s2_send, s2_recv, x_send, x_recv,
):
    c, h = lax.axis_index("ctx"), lax.axis_index("head")
    y = lax.rem(c, 2)
    zl = lax.rem(lax.div(c, 2), 2)
    zh = lax.div(c, 4)
    core = lax.rem(h, 2)
    x = lax.div(h, 2)
    c_y, c_l, c_h = c + 1 - 2 * y, c + 2 - 4 * zl, c + 4 - 8 * zh
    c_hy = c_h + 1 - 2 * y
    h_c, h_x = h + 1 - 2 * core, h + 2 - 4 * x
    h_xc = h_x + 1 - 2 * core
    weights = (wk_ref, wv_ref, wq_ref)
    seqs, span, width = tok_ref.shape
    half = width // 2
    part = span // 2
    rows = seqs * span
    cols = out_ref.shape[2] // 2
    heads = cols // HD

    chunks = [(K, 0), (V, 0), (K, 1), (V, 1), (Q, 0), (Q, 1)]
    local = {}
    for j, g in chunks:
        source = weights[j].at[:, g * cols:(g + 1) * cols]
        local[j, g] = pltpu.make_async_copy(source, wown.at[j, g], l_sem.at[2 * j + g])
        local[j, g].start()

    def strip(r):
        return pl.ds(pl.multiple_of(r * part, part), part)

    own_piece = pltpu.make_async_copy(tok_ref.at[core, strip(x)], atok.at[h], l_sem.at[6])
    own_piece.start()

    barrier = pltpu.get_barrier_semaphore()
    peers = [(c, h_c), (c, h_x), (c, h_xc), (c_y, h), (c_h, h), (c_hy, h), (c_l, h)]
    for peer in peers:
        pl.semaphore_signal(barrier, inc=1, device_id=peer, device_id_type=MESH)
    pl.semaphore_wait(barrier, len(peers))

    pending = []

    def go(src, dst, send, recv, peer):
        copy = pltpu.make_async_remote_copy(
            src_ref=src, dst_ref=dst, send_sem=send, recv_sem=recv, device_id=peer, device_id_type=MESH
        )
        copy.start()
        pending.append(copy)
        return copy

    def a_go(n, s, r, peer):
        return go(tok_ref.at[s, strip(r)], atok.at[h], a_send.at[n], a_recv.at[n], peer)

    a_copies = [
        a_go(0, core, 1 - x, (c, h_x)), a_go(1, 1 - core, 1 - x, (c, h_xc)), a_go(2, 1 - core, x, (c, h_c)),
    ]

    def w_go(j, g):
        local[j, g].wait()
        return go(wown.at[j, g], wpeer.at[j, g], w_send.at[2 * j + g], w_recv.at[2 * j + g], (c_l, h))

    w_copies = {at: w_go(*at) for at in chunks[:2]}
    for copy in a_copies:
        copy.wait_recv()
    own_piece.wait()

    def b_source(zd, yd):
        return atok.at[pl.ds(2 * zd, 2), :, pl.ds(pl.multiple_of(yd * half, half), half)]

    def piece_of(place):
        return tok.at[place, :, core, strip(x)]

    blk, blk_y, blk_h, blk_hy = 2 * zh + y, 2 * zh + 1 - y, 2 * (1 - zh) + y, 2 * (1 - zh) + 1 - y

    def b_go(n, zd, yd, peer):
        return go(b_source(zd, yd), piece_of(blk), b_send.at[n], b_recv.at[n], peer)

    b_y = b_go(0, zh, 1 - y, (c_y, h))
    b_h = b_go(1, 1 - zh, y, (c_h, h))
    b_hy = b_go(2, 1 - zh, 1 - y, (c_hy, h))
    w_copies.update({at: w_go(*at) for at in chunks[2:]})
    tok[blk, :, core, strip(x)] = b_source(zh, y)[...]

    def c_go(n, place):
        return go(piece_of(place), piece_of(place), c_send.at[n], c_recv.at[n], (c, h_x))

    def d_go(n, place):
        mine = tok.at[place, :, core]
        return go(mine, mine, d_send.at[n], d_recv.at[n], (c, h_c))

    def gather_pair(n, first_place, second_place, first_in, second_in):
        if first_in is not None:
            first_in.wait_recv()
        c0 = c_go(n, first_place)
        second_in.wait_recv()
        c1 = c_go(n + 1, second_place)
        c0.wait_recv()
        d0 = d_go(n, first_place)
        c1.wait_recv()
        d1 = d_go(n + 1, second_place)
        d0.wait_recv()
        d1.wait_recv()

    def partial(place, j, g):
        mine = tok[place, zl].reshape(rows, half)
        other = tok[place, 1 - zl].reshape(rows, half)
        return mm(mine, wown[j, g]) + mm(other, wpeer[j, g])

    s1_copies, s2_copies = {}, {}
    arrived = set()

    def first(j, g, slot):
        if (j, g) not in arrived:
            w_copies[j, g].wait_recv()
            arrived.add((j, g))
        here, away = (blk, blk_y) if slot else (blk_h, blk_hy)
        s1_out[j, g, slot] = partial(away, j, g).astype(jnp.bfloat16)
        n = 4 * j + 2 * g + slot
        s1_copies[j, g, slot] = go(
            s1_out.at[j, g, slot], s1_in.at[j, g, slot], s1_send.at[n], s1_recv.at[n], (c_y, h)
        )
        acc[j, g, slot] = partial(here, j, g)

    def second(j, g):
        s1_copies[j, g, 0].wait_recv()
        s2_out[j, g] = (acc[j, g, 0] + s1_in[j, g, 0].astype(jnp.float32)).astype(jnp.bfloat16)
        n = 2 * j + g
        s2_copies[j, g] = go(s2_out.at[j, g], s2_in.at[j, g], s2_send.at[n], s2_recv.at[n], (c_h, h))

    def last(j, g):
        s1_copies[j, g, 1].wait_recv()
        s2_copies[j, g].wait_recv()
        u = acc[j, g, 1] + s1_in[j, g, 1].astype(jnp.float32) + s2_in[j, g].astype(jnp.float32)
        if j != V:
            u = silu(u)
        proj[j, g] = u.astype(jnp.bfloat16)

    def piece(j, g, s, n):
        return proj[j, g, s * span:(s + 1) * span, n * HD:(n + 1) * HD]

    pairs = [(s, n) for s in range(seqs) for n in range(heads)]

    def send_states(step, g, peer):
        scan_out[step, g] = state[g].astype(jnp.bfloat16)
        n = step * 2 + g
        return go(scan_out.at[step, g], scan_in.at[step, g], x_send.at[n], x_recv.at[n], peer)

    x0, x1, x2 = {}, {}, {}

    def states(g):
        last(K, g)
        last(V, g)
        for i, (s, n) in enumerate(pairs):
            state[g, i] = lax.dot_general(
                piece(K, g, s, n), piece(V, g, s, n), (((0,), (0,)), ((), ())), preferred_element_type=jnp.float32
            )
        x0[g] = send_states(0, g, (c_y, h))

    def scan_y(g):
        x0[g].wait_recv()
        state[g] = state[g] + scan_in[0, g].astype(jnp.float32)
        x1[g] = send_states(1, g, (c_l, h))

    def scan_l(g):
        x1[g].wait_recv()
        came = scan_in[1, g].astype(jnp.float32)
        state[g] = state[g] + came
        x2[g] = send_states(2, g, (c_h, h))
        state[g] = came * zl.astype(jnp.float32) + scan_in[0, g].astype(jnp.float32) * y.astype(jnp.float32)

    causal = lax.broadcasted_iota(jnp.int32, (span, span), 0) >= lax.broadcasted_iota(jnp.int32, (span, span), 1)

    def within(g):
        last(Q, g)
        for i, (s, n) in enumerate(pairs):
            scores = lax.dot_general(
                piece(Q, g, s, n), piece(K, g, s, n), (((1,), (1,)), ((), ())), preferred_element_type=jnp.float32
            )
            masked = jnp.where(causal, scores, 0.0).astype(jnp.bfloat16)
            total[g, i] = mm(masked, piece(V, g, s, n))

    def finish(g):
        x2[g].wait_recv()
        for i, (s, n) in enumerate(pairs):
            prefix = state[g, i] + scan_in[2, g, i].astype(jnp.float32) * zh.astype(jnp.float32)
            sums = total[g, i] + mm(piece(Q, g, s, n), prefix.astype(jnp.bfloat16))
            scale_inv = lax.rsqrt(jnp.mean(sums * sums, axis=-1, keepdims=True) + 1e-06)
            at = slice(g * cols + n * HD, g * cols + (n + 1) * HD)
            out_ref[s, :, at] = (sums * scale_inv * gain_ref[:, at]).astype(jnp.bfloat16)

    gather_pair(0, blk, blk_y, None, b_y)
    first(K, 0, 1)
    first(V, 0, 1)
    gather_pair(2, blk_h, blk_hy, b_h, b_hy)
    first(K, 0, 0)
    first(V, 0, 0)
    first(K, 1, 0)
    first(V, 1, 0)
    second(K, 0)
    second(V, 0)
    first(K, 1, 1)
    first(V, 1, 1)
    second(K, 1)
    second(V, 1)
    first(Q, 0, 0)
    states(0)
    first(Q, 0, 1)
    scan_y(0)
    first(Q, 1, 0)
    second(Q, 0)
    states(1)
    first(Q, 1, 1)
    scan_l(0)
    second(Q, 1)
    scan_y(1)
    within(0)
    scan_l(1)
    within(1)
    finish(0)
    finish(1)

    for copy in pending:
        copy.wait_send()


def fused_body(tokens, w_query, w_key, w_value, norm_gain):
    seqs, span, width = tokens.shape
    depth, features = w_query.shape
    rows, half, cols = seqs * span, width // 2, features // 2
    states = seqs * cols // HD
    bf, f32 = jnp.bfloat16, jnp.float32
    dma = pltpu.SemaphoreType.DMA
    sems = [7, 3, 3, 3, 3, 4, 4, 4, 4, 6, 6, 12, 12, 6, 6, 6, 6]
    return pl.pallas_call(
        kernel,
        out_shape=jax.ShapeDtypeStruct((seqs, span, features), bf),
        in_specs=[pl.BlockSpec(memory_space=pltpu.HBM)] * 4 + [pl.BlockSpec(memory_space=pltpu.VMEM)],
        out_specs=pl.BlockSpec(memory_space=pltpu.VMEM),
        scratch_shapes=[
            pltpu.VMEM((4, span // 2, width), bf),
            pltpu.VMEM((4, 2, seqs, span, half), bf),
            pltpu.VMEM((3, 2, depth, cols), bf),
            pltpu.VMEM((3, 2, depth, cols), bf),
            pltpu.VMEM((3, 2, 2, rows, cols), bf),
            pltpu.VMEM((3, 2, 2, rows, cols), bf),
            pltpu.VMEM((3, 2, rows, cols), bf),
            pltpu.VMEM((3, 2, rows, cols), bf),
            pltpu.VMEM((3, 2, 2, rows, cols), f32),
            pltpu.VMEM((3, 2, rows, cols), bf),
            pltpu.VMEM((2, states, HD, HD), f32),
            pltpu.VMEM((3, 2, states, HD, HD), bf),
            pltpu.VMEM((3, 2, states, HD, HD), bf),
            pltpu.VMEM((2, states, span, HD), f32),
        ] + [dma((n,)) for n in sems],
        compiler_params=pltpu.CompilerParams(
            collective_id=0, has_side_effects=True, vmem_limit_bytes=62 * 1024 * 1024
        ),
        cost_estimate=pl.CostEstimate(
            flops=2 * rows * width * 4 * features * 3, bytes_accessed=3 * 2**20, transcendentals=0
        ),
    )(tokens, w_query, w_key, w_value, norm_gain.reshape(1, features))


def solution(mesh):
    in_specs = (
        P(None, "ctx", "head"),
        P("ctx", "head"),
        P("ctx", "head"),
        P("ctx", "head"),
        P("head"),
    )
    out_specs = P(None, "ctx", "head")
    fits = mesh.shape["ctx"] == 8 and mesh.shape["head"] == 4
    body = fused_body if fits else general_body
    return jax.shard_map(body, mesh=mesh, in_specs=in_specs, out_specs=out_specs, check_vma=False)
```

```python
import functools

import jax
import jax.numpy as jnp
from jax import lax
from jax.experimental import pallas as pl
from jax.experimental.pallas import tpu as pltpu
from jax.sharding import PartitionSpec as P

HD = 128
MESH = pl.DeviceIdType.MESH


def entering(part, axis, combine, identity):
    place = lax.axis_index(axis)
    gathered = lax.all_gather(part, axis)
    state = jnp.zeros_like(part) + jnp.asarray(identity, part.dtype)

    def one(hop, state):
        return combine(state, lax.dynamic_index_in_dim(gathered, hop, 0, False))

    return lax.fori_loop(0, place, one, state)


def add_states(earlier, later):
    return earlier + later


def general_body(tokens, w_query, w_key, w_value, norm_gain):
    gathered = lax.all_gather(tokens, "head", axis=2, tiled=True)
    seq_count, span_len, model_dim = gathered.shape
    token_rows = gathered.reshape(seq_count * span_len, model_dim)
    features = w_query.shape[1]
    query_full = lax.all_gather(w_query, "ctx", axis=0, tiled=True)
    query_sum = jnp.dot(token_rows, query_full, preferred_element_type=jnp.float32)
    key_full = lax.all_gather(w_key, "ctx", axis=0, tiled=True)
    key_sum = jnp.dot(token_rows, key_full, preferred_element_type=jnp.float32)
    value_full = lax.all_gather(w_value, "ctx", axis=0, tiled=True)
    value_sum = jnp.dot(token_rows, value_full, preferred_element_type=jnp.float32)
    head_count = features // HD

    def heads_first(projected):
        shaped = projected.astype(jnp.bfloat16).reshape(seq_count, span_len, head_count, HD)
        return shaped.transpose(0, 2, 1, 3)

    query = heads_first(jax.nn.silu(query_sum))
    key_all = heads_first(jax.nn.silu(key_sum))
    value_all = heads_first(value_sum)
    positions = jnp.arange(span_len)
    causal = positions[:, None] >= positions[None, :]
    scores = jnp.einsum("shtd,shud->shtu", query, key_all, preferred_element_type=jnp.float32)
    masked = jnp.where(causal, scores, 0.0).astype(jnp.bfloat16)
    local_out = jnp.einsum("shtu,shud->shtd", masked, value_all, preferred_element_type=jnp.float32)
    states = jnp.einsum("shud,shue->shde", key_all, value_all, preferred_element_type=jnp.float32)
    prefix = entering(states, "ctx", add_states, jnp.zeros_like(states))
    from_prefix = jnp.einsum(
        "shtd,shde->shte", query, prefix.astype(jnp.bfloat16), preferred_element_type=jnp.float32
    )
    total = local_out + from_prefix
    scale_inv = lax.rsqrt(jnp.mean(total * total, axis=-1, keepdims=True) + 1e-06)
    gain_view = norm_gain.reshape(1, head_count, 1, HD)
    normed = total * scale_inv * gain_view
    return normed.transpose(0, 2, 1, 3).reshape(seq_count, span_len, features).astype(jnp.bfloat16)


def silu(u):
    return u / (1.0 + jnp.exp(-u))


def mm(a, b):
    return jnp.dot(a, b, preferred_element_type=jnp.float32)


K, V, Q = 0, 1, 2


def kernel(
    tok_ref, wq_ref, wk_ref, wv_ref, gain_ref, out_ref,
    atok, tok, wown, wpeer, s1_out, s1_in, s2_out, s2_in, acc, proj, state, scan_out, scan_in, total,
    l_sem, a_send, a_recv, b_send, b_recv, c_send, c_recv, d_send, d_recv, w_send, w_recv,
    s1_send, s1_recv, s2_send, s2_recv, x_send, x_recv,
):
    c, h = lax.axis_index("ctx"), lax.axis_index("head")
    y = lax.rem(c, 2)
    zl = lax.rem(lax.div(c, 2), 2)
    zh = lax.div(c, 4)
    core = lax.rem(h, 2)
    x = lax.div(h, 2)
    c_y, c_l, c_h = c + 1 - 2 * y, c + 2 - 4 * zl, c + 4 - 8 * zh
    c_hy = c_h + 1 - 2 * y
    h_c, h_x = h + 1 - 2 * core, h + 2 - 4 * x
    h_xc = h_x + 1 - 2 * core
    weights = (wk_ref, wv_ref, wq_ref)
    seqs, span, width = tok_ref.shape
    half = width // 2
    part = span // 2
    rows = seqs * span
    cols = out_ref.shape[2] // 2
    heads = cols // HD

    chunks = [(K, 0), (V, 0), (K, 1), (V, 1), (Q, 0), (Q, 1)]
    local = {}
    for j, g in chunks:
        source = weights[j].at[:, g * cols:(g + 1) * cols]
        local[j, g] = pltpu.make_async_copy(source, wown.at[j, g], l_sem.at[2 * j + g])
        local[j, g].start()

    def strip(r):
        return pl.ds(pl.multiple_of(r * part, part), part)

    own_piece = pltpu.make_async_copy(tok_ref.at[core, strip(x)], atok.at[h], l_sem.at[6])
    own_piece.start()

    barrier = pltpu.get_barrier_semaphore()
    peers = [(c, h_c), (c, h_x), (c, h_xc), (c_y, h), (c_h, h), (c_hy, h), (c_l, h)]
    for peer in peers:
        pl.semaphore_signal(barrier, inc=1, device_id=peer, device_id_type=MESH)
    pl.semaphore_wait(barrier, len(peers))

    pending = []

    def go(src, dst, send, recv, peer):
        copy = pltpu.make_async_remote_copy(
            src_ref=src, dst_ref=dst, send_sem=send, recv_sem=recv, device_id=peer, device_id_type=MESH
        )
        copy.start()
        pending.append(copy)
        return copy

    def a_go(n, s, r, peer):
        return go(tok_ref.at[s, strip(r)], atok.at[h], a_send.at[n], a_recv.at[n], peer)

    a_copies = [
        a_go(0, core, 1 - x, (c, h_x)), a_go(1, 1 - core, 1 - x, (c, h_xc)), a_go(2, 1 - core, x, (c, h_c)),
    ]

    def w_go(j, g):
        local[j, g].wait()
        return go(wown.at[j, g], wpeer.at[j, g], w_send.at[2 * j + g], w_recv.at[2 * j + g], (c_l, h))

    w_copies = {at: w_go(*at) for at in chunks[:1]}
    for copy in a_copies:
        copy.wait_recv()
    own_piece.wait()

    def b_source(zd, yd):
        return atok.at[pl.ds(2 * zd, 2), :, pl.ds(pl.multiple_of(yd * half, half), half)]

    def piece_of(place):
        return tok.at[place, :, core, strip(x)]

    blk, blk_y, blk_h, blk_hy = 2 * zh + y, 2 * zh + 1 - y, 2 * (1 - zh) + y, 2 * (1 - zh) + 1 - y

    def b_go(n, zd, yd, peer):
        return go(b_source(zd, yd), piece_of(blk), b_send.at[n], b_recv.at[n], peer)

    b_y = b_go(0, zh, 1 - y, (c_y, h))
    b_h = b_go(1, 1 - zh, y, (c_h, h))
    b_hy = b_go(2, 1 - zh, 1 - y, (c_hy, h))
    w_copies[V, 0] = w_go(V, 0)
    tok[blk, :, core, strip(x)] = b_source(zh, y)[...]

    def c_go(n, place):
        return go(piece_of(place), piece_of(place), c_send.at[n], c_recv.at[n], (c, h_x))

    def d_go(n, place):
        mine = tok.at[place, :, core]
        return go(mine, mine, d_send.at[n], d_recv.at[n], (c, h_c))

    def gather_pair(n, first_place, second_place, first_in, second_in, then=()):
        if first_in is not None:
            first_in.wait_recv()
        c0 = c_go(n, first_place)
        second_in.wait_recv()
        c1 = c_go(n + 1, second_place)
        for at in then:
            w_copies[at] = w_go(*at)
        c0.wait_recv()
        d0 = d_go(n, first_place)
        c1.wait_recv()
        d1 = d_go(n + 1, second_place)
        d0.wait_recv()
        d1.wait_recv()

    def partial(place, j, g):
        mine = tok[place, zl].reshape(rows, half)
        other = tok[place, 1 - zl].reshape(rows, half)
        return mm(mine, wown[j, g]) + mm(other, wpeer[j, g])

    s1_copies, s2_copies = {}, {}
    arrived = set()

    def first(j, g, slot):
        if (j, g) not in arrived:
            w_copies[j, g].wait_recv()
            arrived.add((j, g))
        here, away = (blk, blk_y) if slot else (blk_h, blk_hy)
        s1_out[j, g, slot] = partial(away, j, g).astype(jnp.bfloat16)
        n = 4 * j + 2 * g + slot
        s1_copies[j, g, slot] = go(
            s1_out.at[j, g, slot], s1_in.at[j, g, slot], s1_send.at[n], s1_recv.at[n], (c_y, h)
        )
        acc[j, g, slot] = partial(here, j, g)

    def second(j, g):
        s1_copies[j, g, 0].wait_recv()
        s2_out[j, g] = (acc[j, g, 0] + s1_in[j, g, 0].astype(jnp.float32)).astype(jnp.bfloat16)
        n = 2 * j + g
        s2_copies[j, g] = go(s2_out.at[j, g], s2_in.at[j, g], s2_send.at[n], s2_recv.at[n], (c_h, h))

    def last(j, g):
        s1_copies[j, g, 1].wait_recv()
        s2_copies[j, g].wait_recv()
        u = acc[j, g, 1] + s1_in[j, g, 1].astype(jnp.float32) + s2_in[j, g].astype(jnp.float32)
        if j != V:
            u = silu(u)
        proj[j, g] = u.astype(jnp.bfloat16)

    def piece(j, g, s, n):
        return proj[j, g, s * span:(s + 1) * span, n * HD:(n + 1) * HD]

    pairs = [(s, n) for s in range(seqs) for n in range(heads)]

    def send_states(step, g, peer):
        scan_out[step, g] = state[g].astype(jnp.bfloat16)
        n = step * 2 + g
        return go(scan_out.at[step, g], scan_in.at[step, g], x_send.at[n], x_recv.at[n], peer)

    x0, x1, x2 = {}, {}, {}

    def states(g):
        last(K, g)
        last(V, g)
        for i, (s, n) in enumerate(pairs):
            state[g, i] = lax.dot_general(
                piece(K, g, s, n), piece(V, g, s, n), (((0,), (0,)), ((), ())), preferred_element_type=jnp.float32
            )
        x0[g] = send_states(0, g, (c_y, h))

    def scan_y(g):
        x0[g].wait_recv()
        state[g] = state[g] + scan_in[0, g].astype(jnp.float32)
        x1[g] = send_states(1, g, (c_l, h))

    def scan_l(g):
        x1[g].wait_recv()
        came = scan_in[1, g].astype(jnp.float32)
        state[g] = state[g] + came
        x2[g] = send_states(2, g, (c_h, h))
        state[g] = came * zl.astype(jnp.float32) + scan_in[0, g].astype(jnp.float32) * y.astype(jnp.float32)

    causal = lax.broadcasted_iota(jnp.int32, (span, span), 0) >= lax.broadcasted_iota(jnp.int32, (span, span), 1)

    def within(g):
        last(Q, g)
        for i, (s, n) in enumerate(pairs):
            scores = lax.dot_general(
                piece(Q, g, s, n), piece(K, g, s, n), (((1,), (1,)), ((), ())), preferred_element_type=jnp.float32
            )
            masked = jnp.where(causal, scores, 0.0).astype(jnp.bfloat16)
            total[g, i] = mm(masked, piece(V, g, s, n))

    def finish(g):
        x2[g].wait_recv()
        for i, (s, n) in enumerate(pairs):
            prefix = state[g, i] + scan_in[2, g, i].astype(jnp.float32) * zh.astype(jnp.float32)
            sums = total[g, i] + mm(piece(Q, g, s, n), prefix.astype(jnp.bfloat16))
            scale_inv = lax.rsqrt(jnp.mean(sums * sums, axis=-1, keepdims=True) + 1e-06)
            at = slice(g * cols + n * HD, g * cols + (n + 1) * HD)
            out_ref[s, :, at] = (sums * scale_inv * gain_ref[:, at]).astype(jnp.bfloat16)

    gather_pair(0, blk, blk_y, None, b_y)
    first(K, 0, 1)
    first(V, 0, 1)
    gather_pair(2, blk_h, blk_hy, b_h, b_hy, chunks[2:])
    first(K, 0, 0)
    first(V, 0, 0)
    first(K, 1, 0)
    first(V, 1, 0)
    second(K, 0)
    second(V, 0)
    first(K, 1, 1)
    first(V, 1, 1)
    second(K, 1)
    second(V, 1)
    first(Q, 0, 0)
    states(0)
    first(Q, 0, 1)
    scan_y(0)
    first(Q, 1, 0)
    second(Q, 0)
    states(1)
    first(Q, 1, 1)
    scan_l(0)
    second(Q, 1)
    scan_y(1)
    within(0)
    scan_l(1)
    within(1)
    finish(0)
    finish(1)

    for copy in pending:
        copy.wait_send()


def fused_body(tokens, w_query, w_key, w_value, norm_gain):
    seqs, span, width = tokens.shape
    depth, features = w_query.shape
    rows, half, cols = seqs * span, width // 2, features // 2
    states = seqs * cols // HD
    bf, f32 = jnp.bfloat16, jnp.float32
    dma = pltpu.SemaphoreType.DMA
    sems = [7, 3, 3, 3, 3, 4, 4, 4, 4, 6, 6, 12, 12, 6, 6, 6, 6]
    return pl.pallas_call(
        kernel,
        out_shape=jax.ShapeDtypeStruct((seqs, span, features), bf),
        in_specs=[pl.BlockSpec(memory_space=pltpu.HBM)] * 4 + [pl.BlockSpec(memory_space=pltpu.VMEM)],
        out_specs=pl.BlockSpec(memory_space=pltpu.VMEM),
        scratch_shapes=[
            pltpu.VMEM((4, span // 2, width), bf),
            pltpu.VMEM((4, 2, seqs, span, half), bf),
            pltpu.VMEM((3, 2, depth, cols), bf),
            pltpu.VMEM((3, 2, depth, cols), bf),
            pltpu.VMEM((3, 2, 2, rows, cols), bf),
            pltpu.VMEM((3, 2, 2, rows, cols), bf),
            pltpu.VMEM((3, 2, rows, cols), bf),
            pltpu.VMEM((3, 2, rows, cols), bf),
            pltpu.VMEM((3, 2, 2, rows, cols), f32),
            pltpu.VMEM((3, 2, rows, cols), bf),
            pltpu.VMEM((2, states, HD, HD), f32),
            pltpu.VMEM((3, 2, states, HD, HD), bf),
            pltpu.VMEM((3, 2, states, HD, HD), bf),
            pltpu.VMEM((2, states, span, HD), f32),
        ] + [dma((n,)) for n in sems],
        compiler_params=pltpu.CompilerParams(
            collective_id=0, has_side_effects=True, vmem_limit_bytes=62 * 1024 * 1024
        ),
        cost_estimate=pl.CostEstimate(
            flops=2 * rows * width * 4 * features * 3, bytes_accessed=3 * 2**20, transcendentals=0
        ),
    )(tokens, w_query, w_key, w_value, norm_gain.reshape(1, features))


def solution(mesh):
    in_specs = (
        P(None, "ctx", "head"),
        P("ctx", "head"),
        P("ctx", "head"),
        P("ctx", "head"),
        P("head"),
    )
    out_specs = P(None, "ctx", "head")
    fits = mesh.shape["ctx"] == 8 and mesh.shape["head"] == 4
    body = fused_body if fits else general_body
    return jax.shard_map(body, mesh=mesh, in_specs=in_specs, out_specs=out_specs, check_vma=False)
```

```python
import functools

import jax
import jax.numpy as jnp
from jax import lax
from jax.experimental import pallas as pl
from jax.experimental.pallas import tpu as pltpu
from jax.sharding import PartitionSpec as P

HD = 128
MESH = pl.DeviceIdType.MESH


def entering(part, axis, combine, identity):
    place = lax.axis_index(axis)
    gathered = lax.all_gather(part, axis)
    state = jnp.zeros_like(part) + jnp.asarray(identity, part.dtype)

    def one(hop, state):
        return combine(state, lax.dynamic_index_in_dim(gathered, hop, 0, False))

    return lax.fori_loop(0, place, one, state)


def add_states(earlier, later):
    return earlier + later


def general_body(tokens, w_query, w_key, w_value, norm_gain):
    gathered = lax.all_gather(tokens, "head", axis=2, tiled=True)
    seq_count, span_len, model_dim = gathered.shape
    token_rows = gathered.reshape(seq_count * span_len, model_dim)
    features = w_query.shape[1]
    query_full = lax.all_gather(w_query, "ctx", axis=0, tiled=True)
    query_sum = jnp.dot(token_rows, query_full, preferred_element_type=jnp.float32)
    key_full = lax.all_gather(w_key, "ctx", axis=0, tiled=True)
    key_sum = jnp.dot(token_rows, key_full, preferred_element_type=jnp.float32)
    value_full = lax.all_gather(w_value, "ctx", axis=0, tiled=True)
    value_sum = jnp.dot(token_rows, value_full, preferred_element_type=jnp.float32)
    head_count = features // HD

    def heads_first(projected):
        shaped = projected.astype(jnp.bfloat16).reshape(seq_count, span_len, head_count, HD)
        return shaped.transpose(0, 2, 1, 3)

    query = heads_first(jax.nn.silu(query_sum))
    key_all = heads_first(jax.nn.silu(key_sum))
    value_all = heads_first(value_sum)
    positions = jnp.arange(span_len)
    causal = positions[:, None] >= positions[None, :]
    scores = jnp.einsum("shtd,shud->shtu", query, key_all, preferred_element_type=jnp.float32)
    masked = jnp.where(causal, scores, 0.0).astype(jnp.bfloat16)
    local_out = jnp.einsum("shtu,shud->shtd", masked, value_all, preferred_element_type=jnp.float32)
    states = jnp.einsum("shud,shue->shde", key_all, value_all, preferred_element_type=jnp.float32)
    prefix = entering(states, "ctx", add_states, jnp.zeros_like(states))
    from_prefix = jnp.einsum(
        "shtd,shde->shte", query, prefix.astype(jnp.bfloat16), preferred_element_type=jnp.float32
    )
    total = local_out + from_prefix
    scale_inv = lax.rsqrt(jnp.mean(total * total, axis=-1, keepdims=True) + 1e-06)
    gain_view = norm_gain.reshape(1, head_count, 1, HD)
    normed = total * scale_inv * gain_view
    return normed.transpose(0, 2, 1, 3).reshape(seq_count, span_len, features).astype(jnp.bfloat16)


def silu(u):
    return u / (1.0 + jnp.exp(-u))


def mm(a, b):
    return jnp.dot(a, b, preferred_element_type=jnp.float32)


K, V, Q = 0, 1, 2


def kernel(
    tok_ref, wq_ref, wk_ref, wv_ref, gain_ref, out_ref,
    atok, tok, wown, wpeer, s1_out, s1_in, s2_out, s2_in, acc, proj, state, scan_out, scan_in, total,
    l_sem, a_send, a_recv, b_send, b_recv, c_send, c_recv, d_send, d_recv, w_send, w_recv,
    s1_send, s1_recv, s2_send, s2_recv, x_send, x_recv,
):
    c, h = lax.axis_index("ctx"), lax.axis_index("head")
    y = lax.rem(c, 2)
    zl = lax.rem(lax.div(c, 2), 2)
    zh = lax.div(c, 4)
    core = lax.rem(h, 2)
    x = lax.div(h, 2)
    c_y, c_l, c_h = c + 1 - 2 * y, c + 2 - 4 * zl, c + 4 - 8 * zh
    c_hy = c_h + 1 - 2 * y
    z = 2 * zh + zl
    c_m = 6 - 2 * z + y
    h_c, h_x = h + 1 - 2 * core, h + 2 - 4 * x
    h_xc = h_x + 1 - 2 * core
    weights = (wk_ref, wv_ref, wq_ref)
    seqs, span, width = tok_ref.shape
    half = width // 2
    part = span // 2
    rows = seqs * span
    cols = out_ref.shape[2] // 2
    heads = cols // HD

    chunks = [(K, 0), (V, 0), (K, 1), (V, 1), (Q, 0), (Q, 1)]
    local = {}
    for j, g in chunks:
        source = weights[j].at[:, g * cols:(g + 1) * cols]
        local[j, g] = pltpu.make_async_copy(source, wown.at[j, g], l_sem.at[2 * j + g])
        local[j, g].start()

    def strip(r):
        return pl.ds(pl.multiple_of(r * part, part), part)

    own_piece = pltpu.make_async_copy(tok_ref.at[core, strip(x)], atok.at[h], l_sem.at[6])
    own_piece.start()

    barrier = pltpu.get_barrier_semaphore()
    peers = [(c, h_c), (c, h_x), (c, h_xc), (c_y, h), (c_h, h), (c_hy, h), (c_l, h), (c_m, h)]
    for peer in peers:
        pl.semaphore_signal(barrier, inc=1, device_id=peer, device_id_type=MESH)
    pl.semaphore_wait(barrier, len(peers))

    pending = []

    def go(src, dst, send, recv, peer):
        copy = pltpu.make_async_remote_copy(
            src_ref=src, dst_ref=dst, send_sem=send, recv_sem=recv, device_id=peer, device_id_type=MESH
        )
        copy.start()
        pending.append(copy)
        return copy

    def a_go(n, s, r, peer):
        return go(tok_ref.at[s, strip(r)], atok.at[h], a_send.at[n], a_recv.at[n], peer)

    a_copies = [
        a_go(0, core, 1 - x, (c, h_x)), a_go(1, 1 - core, 1 - x, (c, h_xc)), a_go(2, 1 - core, x, (c, h_c)),
    ]

    def w_go(j, g):
        local[j, g].wait()
        return go(wown.at[j, g], wpeer.at[j, g], w_send.at[2 * j + g], w_recv.at[2 * j + g], (c_l, h))

    w_copies = {at: w_go(*at) for at in chunks[:2]}
    for copy in a_copies:
        copy.wait_recv()
    own_piece.wait()

    def b_source(zd, yd):
        return atok.at[pl.ds(2 * zd, 2), :, pl.ds(pl.multiple_of(yd * half, half), half)]

    def piece_of(place):
        return tok.at[place, :, core, strip(x)]

    blk, blk_y, blk_h, blk_hy = 2 * zh + y, 2 * zh + 1 - y, 2 * (1 - zh) + y, 2 * (1 - zh) + 1 - y

    def b_go(n, zd, yd, peer):
        return go(b_source(zd, yd), piece_of(blk), b_send.at[n], b_recv.at[n], peer)

    b_y = b_go(0, zh, 1 - y, (c_y, h))
    b_h = b_go(1, 1 - zh, y, (c_h, h))
    b_hy = b_go(2, 1 - zh, 1 - y, (c_hy, h))
    w_copies.update({at: w_go(*at) for at in chunks[2:]})
    tok[blk, :, core, strip(x)] = b_source(zh, y)[...]

    def c_go(n, place):
        return go(piece_of(place), piece_of(place), c_send.at[n], c_recv.at[n], (c, h_x))

    def d_go(n, place):
        mine = tok.at[place, :, core]
        return go(mine, mine, d_send.at[n], d_recv.at[n], (c, h_c))

    def gather_pair(n, first_place, second_place, first_in, second_in):
        if first_in is not None:
            first_in.wait_recv()
        c0 = c_go(n, first_place)
        second_in.wait_recv()
        c1 = c_go(n + 1, second_place)
        c0.wait_recv()
        d0 = d_go(n, first_place)
        c1.wait_recv()
        d1 = d_go(n + 1, second_place)
        d0.wait_recv()
        d1.wait_recv()

    def partial(place, j, g):
        mine = tok[place, zl].reshape(rows, half)
        other = tok[place, 1 - zl].reshape(rows, half)
        return mm(mine, wown[j, g]) + mm(other, wpeer[j, g])

    s1_copies, s2_copies = {}, {}
    arrived = set()

    def first(j, g, slot):
        if (j, g) not in arrived:
            w_copies[j, g].wait_recv()
            arrived.add((j, g))
        here, away = (blk, blk_y) if slot else (blk_h, blk_hy)
        s1_out[j, g, slot] = partial(away, j, g).astype(jnp.bfloat16)
        n = 4 * j + 2 * g + slot
        s1_copies[j, g, slot] = go(
            s1_out.at[j, g, slot], s1_in.at[j, g, slot], s1_send.at[n], s1_recv.at[n], (c_y, h)
        )
        acc[j, g, slot] = partial(here, j, g)

    def second(j, g):
        s1_copies[j, g, 0].wait_recv()
        s2_out[j, g] = (acc[j, g, 0] + s1_in[j, g, 0].astype(jnp.float32)).astype(jnp.bfloat16)
        n = 2 * j + g
        s2_copies[j, g] = go(s2_out.at[j, g], s2_in.at[j, g], s2_send.at[n], s2_recv.at[n], (c_h, h))

    def last(j, g):
        s1_copies[j, g, 1].wait_recv()
        s2_copies[j, g].wait_recv()
        u = acc[j, g, 1] + s1_in[j, g, 1].astype(jnp.float32) + s2_in[j, g].astype(jnp.float32)
        if j != V:
            u = silu(u)
        proj[j, g] = u.astype(jnp.bfloat16)

    def piece(j, g, s, n):
        return proj[j, g, s * span:(s + 1) * span, n * HD:(n + 1) * HD]

    pairs = [(s, n) for s in range(seqs) for n in range(heads)]

    def send_states(step, g, peer):
        scan_out[step, g] = state[g].astype(jnp.bfloat16)
        n = step * 2 + g
        return go(scan_out.at[step, g], scan_in.at[step, g], x_send.at[n], x_recv.at[n], peer)

    x0 = {}

    def states(g):
        last(K, g)
        last(V, g)
        for i, (s, n) in enumerate(pairs):
            state[g, i] = lax.dot_general(
                piece(K, g, s, n), piece(V, g, s, n), (((0,), (0,)), ((), ())), preferred_element_type=jnp.float32
            )
        x0[g] = send_states(0, g, (c_y, h))

    def up(g):
        return pltpu.make_async_remote_copy(
            src_ref=scan_out.at[1, g], dst_ref=scan_in.at[1, g], send_sem=x_send.at[2 + g],
            recv_sem=x_recv.at[2 + g], device_id=(lax.rem(c + 2, 8), h), device_id_type=MESH,
        )

    def scan_y(g):
        x0[g].wait_recv()
        state[g] = state[g] + scan_in[0, g].astype(jnp.float32)

        @pl.when(z == 0)
        def _():
            scan_in[1, g] = jnp.zeros(scan_in.shape[2:], scan_in.dtype)
            scan_out[1, g] = state[g].astype(jnp.bfloat16)
            up(g).start()

    def scan_z(g):
        @pl.when(z > 0)
        def _():
            up(g).wait_recv()

            @pl.when(z < 3)
            def _():
                scan_out[1, g] = (state[g] + scan_in[1, g].astype(jnp.float32)).astype(jnp.bfloat16)
                up(g).start()

        state[g] = scan_in[1, g].astype(jnp.float32) + scan_in[0, g].astype(jnp.float32) * y.astype(jnp.float32)

    causal = lax.broadcasted_iota(jnp.int32, (span, span), 0) >= lax.broadcasted_iota(jnp.int32, (span, span), 1)

    def within(g):
        last(Q, g)
        for i, (s, n) in enumerate(pairs):
            scores = lax.dot_general(
                piece(Q, g, s, n), piece(K, g, s, n), (((1,), (1,)), ((), ())), preferred_element_type=jnp.float32
            )
            masked = jnp.where(causal, scores, 0.0).astype(jnp.bfloat16)
            total[g, i] = mm(masked, piece(V, g, s, n))

    def finish(g):
        for i, (s, n) in enumerate(pairs):
            sums = total[g, i] + mm(piece(Q, g, s, n), state[g, i].astype(jnp.bfloat16))
            scale_inv = lax.rsqrt(jnp.mean(sums * sums, axis=-1, keepdims=True) + 1e-06)
            at = slice(g * cols + n * HD, g * cols + (n + 1) * HD)
            out_ref[s, :, at] = (sums * scale_inv * gain_ref[:, at]).astype(jnp.bfloat16)

    gather_pair(0, blk, blk_y, None, b_y)
    first(K, 0, 1)
    first(V, 0, 1)
    gather_pair(2, blk_h, blk_hy, b_h, b_hy)
    first(K, 0, 0)
    first(V, 0, 0)
    first(K, 1, 0)
    first(V, 1, 0)
    second(K, 0)
    second(V, 0)
    first(K, 1, 1)
    first(V, 1, 1)
    second(K, 1)
    second(V, 1)
    first(Q, 0, 0)
    states(0)
    first(Q, 0, 1)
    scan_y(0)
    first(Q, 1, 0)
    second(Q, 0)
    states(1)
    first(Q, 1, 1)
    second(Q, 1)
    scan_y(1)
    scan_z(0)
    within(0)
    scan_z(1)
    finish(0)
    within(1)
    finish(1)

    @pl.when(z < 3)
    def _():
        for g in range(2):
            up(g).wait_send()

    for copy in pending:
        copy.wait_send()


def fused_body(tokens, w_query, w_key, w_value, norm_gain):
    seqs, span, width = tokens.shape
    depth, features = w_query.shape
    rows, half, cols = seqs * span, width // 2, features // 2
    states = seqs * cols // HD
    bf, f32 = jnp.bfloat16, jnp.float32
    dma = pltpu.SemaphoreType.DMA
    sems = [7, 3, 3, 3, 3, 4, 4, 4, 4, 6, 6, 12, 12, 6, 6, 4, 4]
    return pl.pallas_call(
        kernel,
        out_shape=jax.ShapeDtypeStruct((seqs, span, features), bf),
        in_specs=[pl.BlockSpec(memory_space=pltpu.HBM)] * 4 + [pl.BlockSpec(memory_space=pltpu.VMEM)],
        out_specs=pl.BlockSpec(memory_space=pltpu.VMEM),
        scratch_shapes=[
            pltpu.VMEM((4, span // 2, width), bf),
            pltpu.VMEM((4, 2, seqs, span, half), bf),
            pltpu.VMEM((3, 2, depth, cols), bf),
            pltpu.VMEM((3, 2, depth, cols), bf),
            pltpu.VMEM((3, 2, 2, rows, cols), bf),
            pltpu.VMEM((3, 2, 2, rows, cols), bf),
            pltpu.VMEM((3, 2, rows, cols), bf),
            pltpu.VMEM((3, 2, rows, cols), bf),
            pltpu.VMEM((3, 2, 2, rows, cols), f32),
            pltpu.VMEM((3, 2, rows, cols), bf),
            pltpu.VMEM((2, states, HD, HD), f32),
            pltpu.VMEM((2, 2, states, HD, HD), bf),
            pltpu.VMEM((2, 2, states, HD, HD), bf),
            pltpu.VMEM((2, states, span, HD), f32),
        ] + [dma((n,)) for n in sems],
        compiler_params=pltpu.CompilerParams(
            collective_id=0, has_side_effects=True, vmem_limit_bytes=62 * 1024 * 1024
        ),
        cost_estimate=pl.CostEstimate(
            flops=2 * rows * width * 4 * features * 3, bytes_accessed=3 * 2**20, transcendentals=0
        ),
    )(tokens, w_query, w_key, w_value, norm_gain.reshape(1, features))


def solution(mesh):
    in_specs = (
        P(None, "ctx", "head"),
        P("ctx", "head"),
        P("ctx", "head"),
        P("ctx", "head"),
        P("head"),
    )
    out_specs = P(None, "ctx", "head")
    fits = mesh.shape["ctx"] == 8 and mesh.shape["head"] == 4
    body = fused_body if fits else general_body
    return jax.shard_map(body, mesh=mesh, in_specs=in_specs, out_specs=out_specs, check_vma=False)
```

```python
import functools

import jax
import jax.numpy as jnp
from jax import lax
from jax.experimental import pallas as pl
from jax.experimental.pallas import tpu as pltpu
from jax.sharding import PartitionSpec as P

HD = 128
MESH = pl.DeviceIdType.MESH


def entering(part, axis, combine, identity):
    place = lax.axis_index(axis)
    gathered = lax.all_gather(part, axis)
    state = jnp.zeros_like(part) + jnp.asarray(identity, part.dtype)

    def one(hop, state):
        return combine(state, lax.dynamic_index_in_dim(gathered, hop, 0, False))

    return lax.fori_loop(0, place, one, state)


def add_states(earlier, later):
    return earlier + later


def general_body(tokens, w_query, w_key, w_value, norm_gain):
    gathered = lax.all_gather(tokens, "head", axis=2, tiled=True)
    seq_count, span_len, model_dim = gathered.shape
    token_rows = gathered.reshape(seq_count * span_len, model_dim)
    features = w_query.shape[1]
    query_full = lax.all_gather(w_query, "ctx", axis=0, tiled=True)
    query_sum = jnp.dot(token_rows, query_full, preferred_element_type=jnp.float32)
    key_full = lax.all_gather(w_key, "ctx", axis=0, tiled=True)
    key_sum = jnp.dot(token_rows, key_full, preferred_element_type=jnp.float32)
    value_full = lax.all_gather(w_value, "ctx", axis=0, tiled=True)
    value_sum = jnp.dot(token_rows, value_full, preferred_element_type=jnp.float32)
    head_count = features // HD

    def heads_first(projected):
        shaped = projected.astype(jnp.bfloat16).reshape(seq_count, span_len, head_count, HD)
        return shaped.transpose(0, 2, 1, 3)

    query = heads_first(jax.nn.silu(query_sum))
    key_all = heads_first(jax.nn.silu(key_sum))
    value_all = heads_first(value_sum)
    positions = jnp.arange(span_len)
    causal = positions[:, None] >= positions[None, :]
    scores = jnp.einsum("shtd,shud->shtu", query, key_all, preferred_element_type=jnp.float32)
    masked = jnp.where(causal, scores, 0.0).astype(jnp.bfloat16)
    local_out = jnp.einsum("shtu,shud->shtd", masked, value_all, preferred_element_type=jnp.float32)
    states = jnp.einsum("shud,shue->shde", key_all, value_all, preferred_element_type=jnp.float32)
    prefix = entering(states, "ctx", add_states, jnp.zeros_like(states))
    from_prefix = jnp.einsum(
        "shtd,shde->shte", query, prefix.astype(jnp.bfloat16), preferred_element_type=jnp.float32
    )
    total = local_out + from_prefix
    scale_inv = lax.rsqrt(jnp.mean(total * total, axis=-1, keepdims=True) + 1e-06)
    gain_view = norm_gain.reshape(1, head_count, 1, HD)
    normed = total * scale_inv * gain_view
    return normed.transpose(0, 2, 1, 3).reshape(seq_count, span_len, features).astype(jnp.bfloat16)


def silu(u):
    return u / (1.0 + jnp.exp(-u))


def mm(a, b):
    return jnp.dot(a, b, preferred_element_type=jnp.float32)


K, V, Q = 0, 1, 2


def kernel(
    tok_ref, wq_ref, wk_ref, wv_ref, gain_ref, out_ref,
    tok, wown, wpeer, s1_out, s1_in, s2_out, s2_in, acc, proj, state, scan_out, scan_in, total,
    l_sem, b_send, b_recv, c_send, c_recv, d_send, d_recv, w_send, w_recv,
    s1_send, s1_recv, s2_send, s2_recv, x_send, x_recv,
):
    c, h = lax.axis_index("ctx"), lax.axis_index("head")
    y = lax.rem(c, 2)
    zl = lax.rem(lax.div(c, 2), 2)
    zh = lax.div(c, 4)
    core = lax.rem(h, 2)
    x = lax.div(h, 2)
    c_y, c_l, c_h = c + 1 - 2 * y, c + 2 - 4 * zl, c + 4 - 8 * zh
    c_hy = c_h + 1 - 2 * y
    z = 2 * zh + zl
    c_m = 6 - 2 * z + y
    h_c, h_x = h + 1 - 2 * core, h + 2 - 4 * x
    h_xc = h_x + 1 - 2 * core
    weights = (wk_ref, wv_ref, wq_ref)
    seqs, span, width = tok_ref.shape
    half = width // 2
    part = span // 2
    rows = seqs * span
    cols = out_ref.shape[2] // 2
    heads = cols // HD

    chunks = [(K, 0), (V, 0), (K, 1), (V, 1), (Q, 0), (Q, 1)]
    local = {}
    for j, g in chunks:
        source = weights[j].at[:, g * cols:(g + 1) * cols]
        local[j, g] = pltpu.make_async_copy(source, wown.at[j, g], l_sem.at[2 * j + g])
        local[j, g].start()

    def strip(r):
        return pl.ds(pl.multiple_of(r * part, part), part)

    barrier = pltpu.get_barrier_semaphore()
    same_zl = [(where, to) for where in (c, c_y, c_h, c_hy) for to in (h, h_c, h_x, h_xc)]
    peers = same_zl[1:] + [(c_l, h), (c_m, h)]
    for peer in peers:
        pl.semaphore_signal(barrier, inc=1, device_id=peer, device_id_type=MESH)
    pl.semaphore_wait(barrier, len(peers))

    pending = []

    def go(src, dst, send, recv, peer):
        copy = pltpu.make_async_remote_copy(
            src_ref=src, dst_ref=dst, send_sem=send, recv_sem=recv, device_id=peer, device_id_type=MESH
        )
        copy.start()
        pending.append(copy)
        return copy

    def w_go(j, g):
        local[j, g].wait()
        return go(wown.at[j, g], wpeer.at[j, g], w_send.at[2 * j + g], w_recv.at[2 * j + g], (c_l, h))

    w_copies = {at: w_go(*at) for at in chunks[:1]}
    blk, blk_y, blk_h, blk_hy = 2 * zh + y, 2 * zh + 1 - y, 2 * (1 - zh) + y, 2 * (1 - zh) + 1 - y
    at_home = x == zh

    def b_copy(n):
        yd, s, r = (1 - y if n & 4 else y), (1 - core if n & 1 else core), (1 - x if n & 2 else x)
        src = tok_ref.at[s, strip(r), pl.ds(pl.multiple_of(yd * half, half), half)]
        dst = tok.at[blk, core, s, strip(r)]
        if n == 0:
            stays = pltpu.make_async_copy(src, dst, l_sem.at[6])
        else:
            stays = None
        goes = pltpu.make_async_remote_copy(
            src_ref=src, dst_ref=dst, send_sem=b_send.at[n], recv_sem=b_recv.at[2 * blk + core],
            device_id=(4 * x + 2 * zl + yd, 2 * r + s), device_id_type=MESH,
        )
        return stays, goes

    for n in (7, 6, 5, 4, 3, 2, 1):
        goes = b_copy(n)[1]
        goes.start()
        pending.append(goes)
    stays, goes = b_copy(0)

    @pl.when(at_home)
    def _():
        stays.start()

    @pl.when(jnp.logical_not(at_home))
    def _():
        goes.start()

    def b_wait(place, own=False):
        for l in range(2):
            dst = tok.at[place, l, core, strip(x)]
            came = pltpu.make_async_remote_copy(
                src_ref=dst, dst_ref=dst, send_sem=b_send.at[0], recv_sem=b_recv.at[2 * place + l],
                device_id=(c, h_c), device_id_type=MESH,
            )
            if not own:
                came.wait_recv()
                continue
            mine = jnp.logical_and(at_home, core == l)

            @pl.when(mine)
            def _():
                stays.wait()

            @pl.when(jnp.logical_not(mine))
            def _():
                came.wait_recv()

    w_copies[V, 0] = w_go(V, 0)

    def piece_of(place):
        return tok.at[place, :, core, strip(x)]

    w_copies.update({at: w_go(*at) for at in chunks[2:]})

    def c_go(n, place):
        return go(piece_of(place), piece_of(place), c_send.at[n], c_recv.at[n], (c, h_x))

    def d_go(n, place):
        mine = tok.at[place, :, core]
        return go(mine, mine, d_send.at[n], d_recv.at[n], (c, h_c))

    def gather_pair(n, first_place, second_place):
        b_wait(first_place, n == 0)
        c0 = c_go(n, first_place)
        b_wait(second_place)
        c1 = c_go(n + 1, second_place)
        c0.wait_recv()
        d0 = d_go(n, first_place)
        c1.wait_recv()
        d1 = d_go(n + 1, second_place)
        d0.wait_recv()
        d1.wait_recv()

    def partial(place, j, g):
        mine = tok[place, zl].reshape(rows, half)
        other = tok[place, 1 - zl].reshape(rows, half)
        return mm(mine, wown[j, g]) + mm(other, wpeer[j, g])

    s1_copies, s2_copies = {}, {}
    arrived = set()

    def first(j, g, slot):
        if (j, g) not in arrived:
            w_copies[j, g].wait_recv()
            arrived.add((j, g))
        here, away = (blk, blk_y) if slot else (blk_h, blk_hy)
        s1_out[j, g, slot] = partial(away, j, g).astype(jnp.bfloat16)
        n = 4 * j + 2 * g + slot
        s1_copies[j, g, slot] = go(
            s1_out.at[j, g, slot], s1_in.at[j, g, slot], s1_send.at[n], s1_recv.at[n], (c_y, h)
        )
        acc[j, g, slot] = partial(here, j, g)

    def second(j, g):
        s1_copies[j, g, 0].wait_recv()
        s2_out[j, g] = (acc[j, g, 0] + s1_in[j, g, 0].astype(jnp.float32)).astype(jnp.bfloat16)
        n = 2 * j + g
        s2_copies[j, g] = go(s2_out.at[j, g], s2_in.at[j, g], s2_send.at[n], s2_recv.at[n], (c_h, h))

    def last(j, g):
        s1_copies[j, g, 1].wait_recv()
        s2_copies[j, g].wait_recv()
        u = acc[j, g, 1] + s1_in[j, g, 1].astype(jnp.float32) + s2_in[j, g].astype(jnp.float32)
        if j != V:
            u = silu(u)
        proj[j, g] = u.astype(jnp.bfloat16)

    def piece(j, g, s, n):
        return proj[j, g, s * span:(s + 1) * span, n * HD:(n + 1) * HD]

    pairs = [(s, n) for s in range(seqs) for n in range(heads)]

    def send_states(step, g, peer):
        scan_out[step, g] = state[g].astype(jnp.bfloat16)
        n = step * 2 + g
        return go(scan_out.at[step, g], scan_in.at[step, g], x_send.at[n], x_recv.at[n], peer)

    x0 = {}

    def states(g):
        last(K, g)
        last(V, g)
        for i, (s, n) in enumerate(pairs):
            state[g, i] = lax.dot_general(
                piece(K, g, s, n), piece(V, g, s, n), (((0,), (0,)), ((), ())), preferred_element_type=jnp.float32
            )
        x0[g] = send_states(0, g, (c_y, h))

    def up(g):
        return pltpu.make_async_remote_copy(
            src_ref=scan_out.at[1, g], dst_ref=scan_in.at[1, g], send_sem=x_send.at[2 + g],
            recv_sem=x_recv.at[2 + g], device_id=(lax.rem(c + 2, 8), h), device_id_type=MESH,
        )

    def scan_y(g):
        x0[g].wait_recv()
        state[g] = state[g] + scan_in[0, g].astype(jnp.float32)

        @pl.when(z == 0)
        def _():
            scan_in[1, g] = jnp.zeros(scan_in.shape[2:], scan_in.dtype)
            scan_out[1, g] = state[g].astype(jnp.bfloat16)
            up(g).start()

    def scan_z(g):
        @pl.when(z > 0)
        def _():
            up(g).wait_recv()

            @pl.when(z < 3)
            def _():
                scan_out[1, g] = (state[g] + scan_in[1, g].astype(jnp.float32)).astype(jnp.bfloat16)
                up(g).start()

        state[g] = scan_in[1, g].astype(jnp.float32) + scan_in[0, g].astype(jnp.float32) * y.astype(jnp.float32)

    causal = lax.broadcasted_iota(jnp.int32, (span, span), 0) >= lax.broadcasted_iota(jnp.int32, (span, span), 1)

    def within(g):
        last(Q, g)
        for i, (s, n) in enumerate(pairs):
            scores = lax.dot_general(
                piece(Q, g, s, n), piece(K, g, s, n), (((1,), (1,)), ((), ())), preferred_element_type=jnp.float32
            )
            masked = jnp.where(causal, scores, 0.0).astype(jnp.bfloat16)
            total[g, i] = mm(masked, piece(V, g, s, n))

    def finish(g):
        for i, (s, n) in enumerate(pairs):
            sums = total[g, i] + mm(piece(Q, g, s, n), state[g, i].astype(jnp.bfloat16))
            scale_inv = lax.rsqrt(jnp.mean(sums * sums, axis=-1, keepdims=True) + 1e-06)
            at = slice(g * cols + n * HD, g * cols + (n + 1) * HD)
            out_ref[s, :, at] = (sums * scale_inv * gain_ref[:, at]).astype(jnp.bfloat16)

    gather_pair(0, blk, blk_y)
    first(K, 0, 1)
    first(V, 0, 1)
    gather_pair(2, blk_h, blk_hy)
    first(K, 0, 0)
    first(V, 0, 0)
    first(K, 1, 0)
    first(V, 1, 0)
    second(K, 0)
    second(V, 0)
    first(K, 1, 1)
    first(V, 1, 1)
    second(K, 1)
    second(V, 1)
    first(Q, 0, 0)
    states(0)
    first(Q, 0, 1)
    scan_y(0)
    first(Q, 1, 0)
    second(Q, 0)
    states(1)
    first(Q, 1, 1)
    second(Q, 1)
    scan_y(1)
    scan_z(0)
    within(0)
    scan_z(1)
    finish(0)
    within(1)
    finish(1)

    @pl.when(z < 3)
    def _():
        for g in range(2):
            up(g).wait_send()

    @pl.when(jnp.logical_not(at_home))
    def _():
        goes.wait_send()

    for copy in pending:
        copy.wait_send()


def fused_body(tokens, w_query, w_key, w_value, norm_gain):
    seqs, span, width = tokens.shape
    depth, features = w_query.shape
    rows, half, cols = seqs * span, width // 2, features // 2
    states = seqs * cols // HD
    bf, f32 = jnp.bfloat16, jnp.float32
    dma = pltpu.SemaphoreType.DMA
    sems = [7, 8, 8, 4, 4, 4, 4, 6, 6, 12, 12, 6, 6, 4, 4]
    return pl.pallas_call(
        kernel,
        out_shape=jax.ShapeDtypeStruct((seqs, span, features), bf),
        in_specs=[pl.BlockSpec(memory_space=pltpu.HBM)] * 4 + [pl.BlockSpec(memory_space=pltpu.VMEM)],
        out_specs=pl.BlockSpec(memory_space=pltpu.VMEM),
        scratch_shapes=[
            pltpu.VMEM((4, 2, seqs, span, half), bf),
            pltpu.VMEM((3, 2, depth, cols), bf),
            pltpu.VMEM((3, 2, depth, cols), bf),
            pltpu.VMEM((3, 2, 2, rows, cols), bf),
            pltpu.VMEM((3, 2, 2, rows, cols), bf),
            pltpu.VMEM((3, 2, rows, cols), bf),
            pltpu.VMEM((3, 2, rows, cols), bf),
            pltpu.VMEM((3, 2, 2, rows, cols), f32),
            pltpu.VMEM((3, 2, rows, cols), bf),
            pltpu.VMEM((2, states, HD, HD), f32),
            pltpu.VMEM((2, 2, states, HD, HD), bf),
            pltpu.VMEM((2, 2, states, HD, HD), bf),
            pltpu.VMEM((2, states, span, HD), f32),
        ] + [dma((n,)) for n in sems],
        compiler_params=pltpu.CompilerParams(
            collective_id=0, has_side_effects=True, vmem_limit_bytes=107 * 512 * 1024
        ),
        cost_estimate=pl.CostEstimate(
            flops=2 * rows * width * 4 * features * 3, bytes_accessed=3 * 2**20, transcendentals=0
        ),
    )(tokens, w_query, w_key, w_value, norm_gain.reshape(1, features))


def solution(mesh):
    in_specs = (
        P(None, "ctx", "head"),
        P("ctx", "head"),
        P("ctx", "head"),
        P("ctx", "head"),
        P("head"),
    )
    out_specs = P(None, "ctx", "head")
    fits = mesh.shape["ctx"] == 8 and mesh.shape["head"] == 4
    body = fused_body if fits else general_body
    return jax.shard_map(body, mesh=mesh, in_specs=in_specs, out_specs=out_specs, check_vma=False)
```

```python
import functools

import jax
import jax.numpy as jnp
from jax import lax
from jax.experimental import pallas as pl
from jax.experimental.pallas import tpu as pltpu
from jax.sharding import PartitionSpec as P

HD = 128
MESH = pl.DeviceIdType.MESH


def entering(part, axis, combine, identity):
    place = lax.axis_index(axis)
    gathered = lax.all_gather(part, axis)
    state = jnp.zeros_like(part) + jnp.asarray(identity, part.dtype)

    def one(hop, state):
        return combine(state, lax.dynamic_index_in_dim(gathered, hop, 0, False))

    return lax.fori_loop(0, place, one, state)


def add_states(earlier, later):
    return earlier + later


def general_body(tokens, w_query, w_key, w_value, norm_gain):
    gathered = lax.all_gather(tokens, "head", axis=2, tiled=True)
    seq_count, span_len, model_dim = gathered.shape
    token_rows = gathered.reshape(seq_count * span_len, model_dim)
    features = w_query.shape[1]
    query_full = lax.all_gather(w_query, "ctx", axis=0, tiled=True)
    query_sum = jnp.dot(token_rows, query_full, preferred_element_type=jnp.float32)
    key_full = lax.all_gather(w_key, "ctx", axis=0, tiled=True)
    key_sum = jnp.dot(token_rows, key_full, preferred_element_type=jnp.float32)
    value_full = lax.all_gather(w_value, "ctx", axis=0, tiled=True)
    value_sum = jnp.dot(token_rows, value_full, preferred_element_type=jnp.float32)
    head_count = features // HD

    def heads_first(projected):
        shaped = projected.astype(jnp.bfloat16).reshape(seq_count, span_len, head_count, HD)
        return shaped.transpose(0, 2, 1, 3)

    query = heads_first(jax.nn.silu(query_sum))
    key_all = heads_first(jax.nn.silu(key_sum))
    value_all = heads_first(value_sum)
    positions = jnp.arange(span_len)
    causal = positions[:, None] >= positions[None, :]
    scores = jnp.einsum("shtd,shud->shtu", query, key_all, preferred_element_type=jnp.float32)
    masked = jnp.where(causal, scores, 0.0).astype(jnp.bfloat16)
    local_out = jnp.einsum("shtu,shud->shtd", masked, value_all, preferred_element_type=jnp.float32)
    states = jnp.einsum("shud,shue->shde", key_all, value_all, preferred_element_type=jnp.float32)
    prefix = entering(states, "ctx", add_states, jnp.zeros_like(states))
    from_prefix = jnp.einsum(
        "shtd,shde->shte", query, prefix.astype(jnp.bfloat16), preferred_element_type=jnp.float32
    )
    total = local_out + from_prefix
    scale_inv = lax.rsqrt(jnp.mean(total * total, axis=-1, keepdims=True) + 1e-06)
    gain_view = norm_gain.reshape(1, head_count, 1, HD)
    normed = total * scale_inv * gain_view
    return normed.transpose(0, 2, 1, 3).reshape(seq_count, span_len, features).astype(jnp.bfloat16)


def silu(u):
    return u / (1.0 + jnp.exp(-u))


def mm(a, b):
    return jnp.dot(a, b, preferred_element_type=jnp.float32)


K, V, Q = 0, 1, 2


def kernel(
    tok_ref, wq_ref, wk_ref, wv_ref, gain_ref, out_ref,
    atok, tok, wown, wpeer, s1_out, s1_in, s2_out, s2_in, acc, proj, state, scan_out, scan_in, total,
    l_sem, a_send, a_recv, b_send, b_recv, c_send, c_recv, d_send, d_recv, w_send, w_recv,
    s1_send, s1_recv, s2_send, s2_recv, x_send, x_recv,
):
    c, h = lax.axis_index("ctx"), lax.axis_index("head")
    y = lax.rem(c, 2)
    zl = lax.rem(lax.div(c, 2), 2)
    zh = lax.div(c, 4)
    core = lax.rem(h, 2)
    x = lax.div(h, 2)
    c_y, c_l, c_h = c + 1 - 2 * y, c + 2 - 4 * zl, c + 4 - 8 * zh
    c_hy = c_h + 1 - 2 * y
    z = 2 * zh + zl
    c_m = 6 - 2 * z + y
    h_c, h_x = h + 1 - 2 * core, h + 2 - 4 * x
    h_xc = h_x + 1 - 2 * core
    weights = (wk_ref, wv_ref, wq_ref)
    seqs, span, width = tok_ref.shape
    half = width // 2
    part = span // 2
    rows = seqs * span
    cols = out_ref.shape[2] // 2
    heads = cols // HD

    chunks = [(K, 0), (V, 0), (K, 1), (V, 1), (Q, 0), (Q, 1)]
    local = {}
    for j, g in chunks:
        source = weights[j].at[:, g * cols:(g + 1) * cols]
        local[j, g] = pltpu.make_async_copy(source, wown.at[j, g], l_sem.at[2 * j + g])
        local[j, g].start()

    def strip(r):
        return pl.ds(pl.multiple_of(r * part, part), part)

    own_piece = pltpu.make_async_copy(tok_ref.at[core, strip(x)], atok.at[h], l_sem.at[6])
    own_piece.start()

    barrier = pltpu.get_barrier_semaphore()
    peers = [(c, h_c), (c, h_x), (c, h_xc), (c_y, h), (c_h, h), (c_hy, h), (c_l, h), (c_m, h)]
    for peer in peers:
        pl.semaphore_signal(barrier, inc=1, device_id=peer, device_id_type=MESH)
    pl.semaphore_wait(barrier, len(peers))

    pending = []

    def go(src, dst, send, recv, peer):
        copy = pltpu.make_async_remote_copy(
            src_ref=src, dst_ref=dst, send_sem=send, recv_sem=recv, device_id=peer, device_id_type=MESH
        )
        copy.start()
        pending.append(copy)
        return copy

    def a_go(n, s, r, peer):
        return go(tok_ref.at[s, strip(r)], atok.at[h], a_send.at[n], a_recv.at[n], peer)

    a_copies = [
        a_go(0, core, 1 - x, (c, h_x)), a_go(1, 1 - core, 1 - x, (c, h_xc)), a_go(2, 1 - core, x, (c, h_c)),
    ]

    def w_go(j, g):
        local[j, g].wait()
        return go(wown.at[j, g], wpeer.at[j, g], w_send.at[2 * j + g], w_recv.at[2 * j + g], (c_l, h))

    w_copies = {at: w_go(*at) for at in chunks[:2]}
    for copy in a_copies:
        copy.wait_recv()
    own_piece.wait()

    def b_source(zd, yd):
        return atok.at[pl.ds(2 * zd, 2), :, pl.ds(pl.multiple_of(yd * half, half), half)]

    def piece_of(place):
        return tok.at[place, :, core, strip(x)]

    blk, blk_y, blk_h, blk_hy = 2 * zh + y, 2 * zh + 1 - y, 2 * (1 - zh) + y, 2 * (1 - zh) + 1 - y

    def b_go(n, zd, yd, peer):
        return go(b_source(zd, yd), piece_of(blk), b_send.at[n], b_recv.at[n], peer)

    b_y = b_go(0, zh, 1 - y, (c_y, h))
    b_h = b_go(1, 1 - zh, y, (c_h, h))
    b_hy = b_go(2, 1 - zh, 1 - y, (c_hy, h))
    w_copies.update({at: w_go(*at) for at in chunks[2:]})
    tok[blk, :, core, strip(x)] = b_source(zh, y)[...]

    def c_go(n, place):
        return go(piece_of(place), piece_of(place), c_send.at[n], c_recv.at[n], (c, h_x))

    def d_go(n, place):
        mine = tok.at[place, :, core]
        return go(mine, mine, d_send.at[n], d_recv.at[n], (c, h_c))

    def gather_pair(n, first_place, second_place, first_in, second_in):
        if first_in is not None:
            first_in.wait_recv()
        c0 = c_go(n, first_place)
        second_in.wait_recv()
        c1 = c_go(n + 1, second_place)
        c0.wait_recv()
        d0 = d_go(n, first_place)
        c1.wait_recv()
        d1 = d_go(n + 1, second_place)
        d0.wait_recv()
        d1.wait_recv()

    def partial(place, j, g):
        mine = tok[place, zl].reshape(rows, half)
        other = tok[place, 1 - zl].reshape(rows, half)
        return mm(mine, wown[j, g]) + mm(other, wpeer[j, g])

    s1_copies, s2_copies = {}, {}
    arrived = set()

    def first(j, g, slot):
        if (j, g) not in arrived:
            w_copies[j, g].wait_recv()
            arrived.add((j, g))
        here, away = (blk, blk_y) if slot else (blk_h, blk_hy)
        s1_out[j, g, slot] = partial(away, j, g).astype(jnp.bfloat16)
        n = 4 * j + 2 * g + slot
        s1_copies[j, g, slot] = go(
            s1_out.at[j, g, slot], s1_in.at[j, g, slot], s1_send.at[n], s1_recv.at[n], (c_y, h)
        )
        acc[j, g, slot] = partial(here, j, g)

    def second(j, g):
        s1_copies[j, g, 0].wait_recv()
        s2_out[j, g] = (acc[j, g, 0] + s1_in[j, g, 0].astype(jnp.float32)).astype(jnp.bfloat16)
        n = 2 * j + g
        s2_copies[j, g] = go(s2_out.at[j, g], s2_in.at[j, g], s2_send.at[n], s2_recv.at[n], (c_h, h))

    def last(j, g):
        s1_copies[j, g, 1].wait_recv()
        s2_copies[j, g].wait_recv()
        u = acc[j, g, 1] + s1_in[j, g, 1].astype(jnp.float32) + s2_in[j, g].astype(jnp.float32)
        if j != V:
            u = silu(u)
        proj[j, g] = u.astype(jnp.bfloat16)

    def piece(j, g, s, n):
        return proj[j, g, s * span:(s + 1) * span, n * HD:(n + 1) * HD]

    pairs = [(s, n) for s in range(seqs) for n in range(heads)]

    def send_states(step, g, peer):
        scan_out[step, g] = state[g].astype(jnp.bfloat16)
        n = step * 2 + g
        return go(scan_out.at[step, g], scan_in.at[step, g], x_send.at[n], x_recv.at[n], peer)

    x0 = {}

    def states(g):
        last(K, g)
        last(V, g)
        for i, (s, n) in enumerate(pairs):
            state[g, i] = lax.dot_general(
                piece(K, g, s, n), piece(V, g, s, n), (((0,), (0,)), ((), ())), preferred_element_type=jnp.float32
            )
        x0[g] = send_states(0, g, (c_y, h))

    def up(g):
        return pltpu.make_async_remote_copy(
            src_ref=scan_out.at[1, g], dst_ref=scan_in.at[1, g], send_sem=x_send.at[2 + g],
            recv_sem=x_recv.at[2 + g], device_id=(lax.rem(c + 2, 8), h), device_id_type=MESH,
        )

    def scan_y(g):
        x0[g].wait_recv()
        state[g] = state[g] + scan_in[0, g].astype(jnp.float32)

        @pl.when(z == 0)
        def _():
            scan_in[1, g] = jnp.zeros(scan_in.shape[2:], scan_in.dtype)
            scan_out[1, g] = state[g].astype(jnp.bfloat16)
            up(g).start()

    def scan_z(g):
        @pl.when(z > 0)
        def _():
            up(g).wait_recv()

            @pl.when(z < 3)
            def _():
                scan_out[1, g] = (state[g] + scan_in[1, g].astype(jnp.float32)).astype(jnp.bfloat16)
                up(g).start()

        state[g] = scan_in[1, g].astype(jnp.float32) + scan_in[0, g].astype(jnp.float32) * y.astype(jnp.float32)

    causal = lax.broadcasted_iota(jnp.int32, (span, span), 0) >= lax.broadcasted_iota(jnp.int32, (span, span), 1)

    def within(g):
        last(Q, g)
        for i, (s, n) in enumerate(pairs):
            scores = lax.dot_general(
                piece(Q, g, s, n), piece(K, g, s, n), (((1,), (1,)), ((), ())), preferred_element_type=jnp.float32
            )
            masked = jnp.where(causal, scores, 0.0).astype(jnp.bfloat16)
            total[g, i] = mm(masked, piece(V, g, s, n))

    def finish(g):
        for i, (s, n) in enumerate(pairs):
            sums = total[g, i] + mm(piece(Q, g, s, n), state[g, i].astype(jnp.bfloat16))
            scale_inv = lax.rsqrt(jnp.mean(sums * sums, axis=-1, keepdims=True) + 1e-06)
            at = slice(g * cols + n * HD, g * cols + (n + 1) * HD)
            out_ref[s, :, at] = (sums * scale_inv * gain_ref[:, at]).astype(jnp.bfloat16)

    gather_pair(0, blk, blk_y, None, b_y)
    first(K, 0, 1)
    first(V, 0, 1)
    gather_pair(2, blk_h, blk_hy, b_h, b_hy)
    first(K, 0, 0)
    first(V, 0, 0)
    first(K, 1, 0)
    first(V, 1, 0)
    second(K, 0)
    second(V, 0)
    first(K, 1, 1)
    first(V, 1, 1)
    second(K, 1)
    second(V, 1)
    first(Q, 0, 0)
    states(0)
    first(Q, 0, 1)
    scan_y(0)
    first(Q, 1, 0)
    second(Q, 0)
    states(1)
    first(Q, 1, 1)
    second(Q, 1)
    scan_y(1)
    scan_z(0)
    within(0)
    scan_z(1)
    finish(0)
    within(1)
    finish(1)

    @pl.when(z < 3)
    def _():
        for g in range(2):
            up(g).wait_send()

    for copy in pending:
        copy.wait_send()


def fused_body(tokens, w_query, w_key, w_value, norm_gain):
    seqs, span, width = tokens.shape
    depth, features = w_query.shape
    rows, half, cols = seqs * span, width // 2, features // 2
    states = seqs * cols // HD
    bf, f32 = jnp.bfloat16, jnp.float32
    dma = pltpu.SemaphoreType.DMA
    sems = [7, 3, 3, 3, 3, 4, 4, 4, 4, 6, 6, 12, 12, 6, 6, 4, 4]
    return pl.pallas_call(
        kernel,
        out_shape=jax.ShapeDtypeStruct((seqs, span, features), bf),
        in_specs=[pl.BlockSpec(memory_space=pltpu.HBM)] * 4 + [pl.BlockSpec(memory_space=pltpu.VMEM)],
        out_specs=pl.BlockSpec(memory_space=pltpu.VMEM),
        scratch_shapes=[
            pltpu.VMEM((4, span // 2, width), bf),
            pltpu.VMEM((4, 2, seqs, span, half), bf),
            pltpu.VMEM((3, 2, depth, cols), bf),
            pltpu.VMEM((3, 2, depth, cols), bf),
            pltpu.VMEM((3, 2, 2, rows, cols), bf),
            pltpu.VMEM((3, 2, 2, rows, cols), bf),
            pltpu.VMEM((3, 2, rows, cols), bf),
            pltpu.VMEM((3, 2, rows, cols), bf),
            pltpu.VMEM((3, 2, 2, rows, cols), f32),
            pltpu.VMEM((3, 2, rows, cols), bf),
            pltpu.VMEM((2, states, HD, HD), f32),
            pltpu.VMEM((2, 2, states, HD, HD), bf),
            pltpu.VMEM((2, 2, states, HD, HD), bf),
            pltpu.VMEM((2, states, span, HD), f32),
        ] + [dma((n,)) for n in sems],
        compiler_params=pltpu.CompilerParams(
            collective_id=0, has_side_effects=True, vmem_limit_bytes=107 * 512 * 1024
        ),
        cost_estimate=pl.CostEstimate(
            flops=2 * rows * width * 4 * features * 3, bytes_accessed=3 * 2**20, transcendentals=0
        ),
    )(tokens, w_query, w_key, w_value, norm_gain.reshape(1, features))


def solution(mesh):
    in_specs = (
        P(None, "ctx", "head"),
        P("ctx", "head"),
        P("ctx", "head"),
        P("ctx", "head"),
        P("head"),
    )
    out_specs = P(None, "ctx", "head")
    fits = mesh.shape["ctx"] == 8 and mesh.shape["head"] == 4
    body = fused_body if fits else general_body
    return jax.shard_map(body, mesh=mesh, in_specs=in_specs, out_specs=out_specs, check_vma=False)
```
